128 devices in a mesh: cfg: 8 (over y_hi, z), mode: 16 (over y_lo, x, core).
Axes of the slice: x: 4, y: 4 (y_hi: 2, y_lo: 2; y = y_hi * 2 + y_lo), z: 4, core: 2. Of those that a mesh axis runs over, the one named last changes fastest.
Arguments:
- coords: bfloat16 [10368, 4096], P('mode', 'cfg'), may hold values from -6 to 6
- curvature: float32 [10368], P('mode'), may hold values from 0.2 to 5
- weight: float32 [10368], P('mode'), may hold values from 0.3 to 3
- polar: bfloat16 [10368, 10368], P('mode'), may hold values from -0.078125 to 0.078125
- forces: bfloat16 [10368, 4096], P('mode', 'cfg'), may hold values from -6 to 6
Outputs:
- gradient: float32 [10368, 10368], P('cfg', 'mode')
The draws below stay inside these ranges and needn't reach their ends.
All inputs are finite; a program needn't handle non-finite values.
Results may differ from the reference program's by a relative error of at most 0.019.
Values may be sent and summed in bfloat16 or wider, within the bound.
No kernel may reach another device: no remote copies, remote signals or barrier semaphores. Data moves between devices by JAX's collectives and lax.ppermute only.
A program may use at most 128 MiB of HBM per device.

```python
import math
import jax
import jax.numpy as jnp
from jax import lax

M = 10368
CFG_DEV = 512
CONFIGS = 4096
N_CFG = 8
N_MODE = 16


def with_spikes(values, key, source, target, blocks, factor):
    owner, partner = [(jnp.arange(values.shape[dim]) // (values.shape[dim] // blocks)).reshape([-1 if axis == dim else 1 for axis in range(values.ndim)]) for dim in (source, target)]
    chosen = jax.random.permutation(key, blocks)[partner]
    strong = (owner == chosen) | (owner == (partner + blocks // 2) % blocks)
    return jnp.where(strong, factor * values, values)


def block_scale(rng, extent, cuts, least, top_value):
    factor_of, own = 1.0, jax.random.fold_in(rng, 6)
    for dim, blocks in cuts:
        heights = jnp.exp(jax.random.uniform(jax.random.fold_in(own, dim), (blocks,), jnp.float32, least / len(cuts), top_value / len(cuts)))
        factor_of = factor_of * jnp.repeat(heights, extent[dim] // blocks).reshape([-1 if axis == dim else 1 for axis in range(len(extent))])
    return factor_of


def normal_values(own_key, dims, width, bound, cuts=(), held_as=jnp.bfloat16):
    loudness = block_scale(own_key, dims, cuts, -0.22, 0.18) if cuts else 1.0
    entries = jax.random.normal(own_key, dims, jnp.float32) * width * loudness
    return jnp.minimum(jnp.maximum(entries, -bound), bound).astype(held_as)


def noise_with(key, shape, deviation, limit, cuts, heavy, dtype=jnp.bfloat16):
    entries = deviation * jax.random.normal(key, shape, jnp.float32)
    if cuts:
        entries = entries * block_scale(key, shape, cuts, -0.22, 0.18)
    return jnp.clip(with_spikes(entries, jax.random.fold_in(key, 3), *heavy), -limit, limit).astype(dtype)


def setup_inputs(seed: int = 0) -> dict:
    key_list = jax.random.split(jax.random.key(seed), 6)
    return {
        "coords": normal_values(key_list[0], (M, CONFIGS), 1.0, 6.0, ((0, 16), (1, 8))),
        "curvature": jnp.clip(jnp.exp(math.log(5.0) - 3.218876 * jax.random.uniform(key_list[1], (M,), jnp.float32) ** block_scale(key_list[1], (M,), ((0, 16),), -0.2, 0.2)), 0.2, 5.0),
        "weight": jnp.clip(jnp.exp(math.log(3.0) - 2.3025851 * jax.random.uniform(key_list[2], (M,), jnp.float32) ** block_scale(key_list[2], (M,), ((0, 16),), -0.2, 0.2)), 0.3, 3.0),
        "polar": noise_with(key_list[3], (M, M), M ** -0.5, 0.078125, ((0, 16),), (0, 1, 16, 2.0)),
        "forces": normal_values(key_list[4], (M, CONFIGS), 1.0, 6.0, ((0, 16), (1, 8))),
    }


def reference(coords, curvature, weight, polar, forces):
    f32 = jnp.float32
    bf16 = jnp.bfloat16
    block_modes = M // N_MODE
    scaled = (coords.astype(f32) * curvature[:, None]).astype(bf16)
    weighted = (coords.astype(f32) * weight[:, None]).astype(bf16)
    scaled_blocks = scaled.reshape(N_MODE, block_modes, CONFIGS)
    polar_blocks = polar.reshape(N_MODE, block_modes, M)

    def harmonic_step(total, pieces):
        scaled_piece, polar_piece = pieces
        term = jnp.dot(polar_piece.astype(f32).T, scaled_piece.astype(f32))
        rounded = lax.optimization_barrier(term.astype(bf16))
        return (total + rounded.astype(f32), 0)
    harmonic, unused = lax.scan(harmonic_step, jnp.zeros((M, CONFIGS), f32), (scaled_blocks, polar_blocks))
    residual = (forces.astype(f32) + harmonic).astype(bf16)
    factor = 1.0 / math.sqrt(CONFIGS)
    resid_blocks = residual.reshape(M, N_CFG, CFG_DEV).transpose(1, 0, 2)
    weight_blocks = weighted.reshape(M, N_CFG, CFG_DEV).transpose(1, 0, 2)

    def gradient_step(total, pieces):
        resid_piece, weight_piece = pieces
        term = jnp.dot(resid_piece.astype(f32), weight_piece.astype(f32).T) * factor
        rounded = lax.optimization_barrier(term.astype(bf16))
        return (total + rounded.astype(f32), 0)
    gradient, unused_two = lax.scan(gradient_step, jnp.zeros((M, M), f32), (resid_blocks, weight_blocks))
    return gradient
```

```python
import math

import jax
import jax.numpy as jnp
from jax import lax
from jax.experimental import pallas as pl
from jax.experimental.pallas import tpu as pltpu
from jax.sharding import PartitionSpec as P

F32 = jnp.float32
BF16 = jnp.bfloat16
X, Z = 4, 4
Q = 128
CHUNKS = (((0, 0),), ((0, 3), (0, 1)), ((1, 0), (1, 3), (1, 1)), ((0, 2), (1, 2)))


def mode_perm(fn):
    out = []
    for j in range(16):
        yl, x, k = j // 8, (j // 2) % 4, j % 2
        a, b, c = fn(yl, x, k)
        out.append((j, (a * 4 + b) * 2 + c))
    return out


FIRST = mode_perm(lambda yl, x, k: (yl, x ^ (3 if k else 1), k))
SECOND = mode_perm(lambda yl, x, k: (yl, x ^ (1 if k else 3), k))
YSWAP = mode_perm(lambda yl, x, k: (1 - yl, x, k))
KSWAP = mode_perm(lambda yl, x, k: (yl, x, 1 - k))


def cfg_perm(dy, dz):
    return [(c, (c // 4 ^ dy) * 4 + (c % 4 + dz) % 4) for c in range(8)]


TRANSPOSE = [(i * 16 + J * 2 + k, J * 16 + i * 2 + k) for i in range(8) for J in range(8) for k in range(2)]


def reorder(v):
    return jnp.concatenate([v[:, :Q], v[:, 2 * Q : 3 * Q], v[:, Q : 2 * Q], v[:, 3 * Q :]], axis=1)


def mm1_body(n, flags, po, px, f, *refs):
    units, (keep, s2, s1) = refs[: 2 * n], refs[2 * n :]
    for u in range(n):
        co, cx = units[2 * u], units[2 * u + 1]
        h = jnp.dot(po[...], co[...], preferred_element_type=F32)
        h += jnp.dot(px[...], reorder(cx[...]), preferred_element_type=F32)
        h += f[...].astype(F32) * flags[u].astype(F32)
        h = h.astype(BF16)
        a = slice(u * Q, (u + 1) * Q)
        b = slice((n + u) * Q, (n + u + 1) * Q)
        keep[:, a] = h[:, :Q]
        s2[:, a] = h[:, Q : 2 * Q]
        s1[:, a] = h[:, 2 * Q : 3 * Q]
        s1[:, b] = h[:, 3 * Q :]


VM = pl.BlockSpec(memory_space=pltpu.VMEM)
SM = pl.BlockSpec(memory_space=pltpu.SMEM)
PARAMS = pltpu.CompilerParams(vmem_limit_bytes=48 * 1024 * 1024)


def mm1(flags, po, px, f, units):
    n = len(units)
    rows = po.shape[0]
    depth = po.shape[1] * 2
    flat = [v for u in units for v in u]
    return pl.pallas_call(
        lambda *r: mm1_body(n, *r),
        out_shape=[jax.ShapeDtypeStruct((rows, w * n * Q), BF16) for w in (1, 1, 2)],
        in_specs=[SM] + [VM] * (3 + 2 * n),
        out_specs=[VM] * 3,
        compiler_params=PARAMS,
        cost_estimate=pl.CostEstimate(
            flops=2 * rows * depth * 4 * Q * n, bytes_accessed=2 * rows * (depth + Q * 12 * n), transcendentals=0
        ),
        name="mm1",
    )(flags, po, px, f, *flat)


def mm2_body(n, first, swap, *refs):
    refs = list(refs)
    acc = None if first else refs.pop(0)
    r, units, out = refs[:4], refs[4 : 4 + n], refs[4 + n]
    total = None if first else acc[...]
    for u in range(n):
        a = slice(u * Q, (u + 1) * Q)
        order = (0, 2, 1, 3) if swap else (0, 1, 2, 3)
        ru = jnp.concatenate([r[s][:, a] for s in order], axis=1)
        t = lax.dot_general(ru, units[u][...], (((1,), (1,)), ((), ())), preferred_element_type=F32)
        total = t if total is None else total + t
    out[...] = total.astype(out.dtype)


def mm2(acc, r, units, swap, dtype=F32):
    n = len(units)
    rows, cols = r[0].shape[0], units[0].shape[0]
    first = acc is None
    args = ([] if first else [acc]) + list(r) + list(units)
    return pl.pallas_call(
        lambda *a: mm2_body(n, first, swap, *a),
        out_shape=jax.ShapeDtypeStruct((rows, cols), dtype),
        in_specs=[VM] * len(args),
        out_specs=VM,
        compiler_params=PARAMS,
        cost_estimate=pl.CostEstimate(
            flops=2 * rows * cols * 4 * Q * n, bytes_accessed=8 * rows * cols + 2 * rows * Q * 8 * n, transcendentals=0
        ),
        name="mm2",
    )(*args)


def on_device(coords, curvature, weight, polar, forces):
    i, j = lax.axis_index("cfg"), lax.axis_index("mode")
    yh, z = i // Z, i % Z
    k, x, chip = j % 2, (j // 2) % X, j // 2
    rows = coords.shape[0]

    second, first = jnp.where(k == 0, 3, 1), jnp.where(k == 0, 1, 3)
    order = [x, x ^ second, x ^ first, x ^ 2]

    def mine(v):
        return jnp.concatenate([lax.dynamic_slice_in_dim(v, o * Q, Q, axis=1) for o in order], axis=1)

    def half(which):
        part = lax.dynamic_slice_in_dim(polar, (2 * i + which) * rows, rows, axis=1)
        return (part.astype(F32) * curvature[:, None]).astype(BF16).T

    px = lax.ppermute(half(1 - k), "mode", KSWAP)
    po = half(k)

    unit = {}
    unit[0, 0] = mine(coords)
    unit[1, 0] = lax.ppermute(unit[0, 0], "cfg", cfg_perm(1, 0))
    for dz in (3, 1, 2):
        unit[0, dz] = lax.ppermute(unit[0, 0], "cfg", cfg_perm(0, -dz))
    for dz in (3, 1, 2):
        unit[1, dz] = lax.ppermute(unit[1, 0], "cfg", cfg_perm(0, -dz))
    other = {u: lax.ppermute(v, "mode", KSWAP) for u, v in unit.items()}

    f_own = mine(forces)
    f_all = mine(lax.ppermute(forces, ("cfg", "mode"), TRANSPOSE))

    acc_own = acc_oth = None
    for number, chunk in enumerate(CHUNKS):
        n = len(chunk)
        flags = jnp.stack([((yh ^ dy) * Z + (z + dz) % Z == chip).astype(jnp.int32) for dy, dz in chunk])
        keep, s2, s1 = mm1(flags, po, px, f_own if number == 0 else f_all, [(unit[u], other[u]) for u in chunk])
        g1 = lax.ppermute(s1, "mode", FIRST)
        s2 = (s2.astype(F32) + g1[:, n * Q :].astype(F32)).astype(BF16)
        g2 = lax.ppermute(s2, "mode", SECOND)
        s3 = (keep.astype(F32) + g1[:, : n * Q].astype(F32) + g2.astype(F32)).astype(BF16)
        g3 = lax.ppermute(s3, "mode", YSWAP)
        r0 = (s3.astype(F32) + g3.astype(F32)).astype(BF16)
        r1 = lax.ppermute(r0, "mode", SECOND)
        r2 = lax.ppermute(r0, "mode", FIRST)
        r3 = lax.ppermute(r1, "mode", FIRST)
        r = (r0, r1, r2, r3)
        last = number == len(CHUNKS) - 1
        acc_oth = mm2(acc_oth, r, [other[u] for u in chunk], True, BF16 if last else F32)
        if last:
            got = lax.ppermute(acc_oth, "mode", KSWAP)
        acc_own = mm2(acc_own, r, [unit[u] for u in chunk], False)

    factor = weight[None, :] * (1.0 / math.sqrt(coords.shape[1] * lax.axis_size("cfg")))
    got = got.astype(F32)
    both = jnp.where(k == 0, jnp.concatenate([acc_own, got], axis=0), jnp.concatenate([got, acc_own], axis=0))
    return both * factor


def solution(mesh):
    placed = (P("mode", "cfg"), P("mode"), P("mode"), P("mode", None), P("mode", "cfg"))
    return jax.shard_map(
        on_device, mesh=mesh, in_specs=placed, out_specs=P("cfg", "mode"), check_vma=False
    )
```

```python
import math

import jax
import jax.numpy as jnp
from jax import lax
from jax.experimental import pallas as pl
from jax.experimental.pallas import tpu as pltpu
from jax.sharding import PartitionSpec as P

F32 = jnp.float32
BF16 = jnp.bfloat16
X, Z = 4, 4
Q = 128
CHUNKS = (((0, 0),), ((0, 3), (0, 1), (1, 0)), ((1, 3), (1, 1)), ((0, 2), (1, 2)))
STEPS = (
    "M0 S0 Y0 G0 R0 M1 F0 S1 G1 M2 T0 Y1 S2 G2 M3 R1 Y2 S3 F1 R2 Y3 F2 R3 T1 F3 T2 T3".split()
)


def mode_perm(fn):
    out = []
    for j in range(16):
        yl, x, k = j // 8, (j // 2) % 4, j % 2
        a, b, c = fn(yl, x, k)
        out.append((j, (a * 4 + b) * 2 + c))
    return out


FIRST = mode_perm(lambda yl, x, k: (yl, x ^ (3 if k else 1), k))
SECOND = mode_perm(lambda yl, x, k: (yl, x ^ (1 if k else 3), k))
YSWAP = mode_perm(lambda yl, x, k: (1 - yl, x, k))
KSWAP = mode_perm(lambda yl, x, k: (yl, x, 1 - k))


def all_perm(fn):
    out = []
    for d in range(128):
        src = (d // 64, (d // 16) % 4, (d // 8) % 2, (d // 2) % 4, d % 2)
        a, b, c, e, k = fn(*src)
        out.append((d, (((a * 4 + b) * 2 + c) * 4 + e) * 2 + k))
    return out


def cfg_perm(dy, dz):
    return [(c, (c // 4 ^ dy) * 4 + (c % 4 + dz) % 4) for c in range(8)]


ONWARD = all_perm(lambda yh, z, yl, x, k: (yh, (z + (3 if k else 1)) % 4, yl, x, k))
FORCES = all_perm(lambda yh, z, yl, x, k: (yl, x, yh, (x + z) % 4, k))

VM = pl.BlockSpec(memory_space=pltpu.VMEM)
SM = pl.BlockSpec(memory_space=pltpu.SMEM)
ANY = pl.BlockSpec(memory_space=pl.ANY)
HBM = pl.BlockSpec(memory_space=pltpu.HBM)
TOKEN = jax.ShapeDtypeStruct((8, 128), F32)


class Chain:
    def __init__(self):
        self.token = None

    def __call__(self, name, body, outs, args, specs, out_specs=None, aliases=None, scratch=(), mib=4):
        given = self.token is not None
        n_in, n_out = len(args), len(outs)

        def kernel(*refs):
            ins = refs[:n_in]
            rest = refs[n_in + int(given) :]
            rest[n_out][...] = jnp.zeros((8, 128), F32)
            body(ins, rest[:n_out], rest[n_out + 1 :])

        res = pl.pallas_call(
            kernel,
            out_shape=list(outs) + [TOKEN],
            in_specs=list(specs) + ([ANY] if given else []),
            out_specs=(list(out_specs) if out_specs else [VM] * n_out) + [VM],
            input_output_aliases=aliases or {},
            scratch_shapes=list(scratch),
            compiler_params=pltpu.CompilerParams(vmem_limit_bytes=mib * 1024 * 1024),
            cost_estimate=pl.CostEstimate(flops=1000, bytes_accessed=1000, transcendentals=0),
            name=name,
        )(*args, *([self.token] if given else []))
        self.token = res[-1]
        return res[:-1]


def like(v):
    return jax.ShapeDtypeStruct(v.shape, v.dtype)


def wide(v):
    return v.astype(F32)


def reorder(v):
    return jnp.concatenate([v[:, :Q], v[:, 2 * Q : 3 * Q], v[:, Q : 2 * Q], v[:, 3 * Q :]], axis=1)


def on_device(coords, curvature, weight, polar, forces):
    i, j = lax.axis_index("cfg"), lax.axis_index("mode")
    yh, z = i // Z, i % Z
    k, x, chip, yl = j % 2, (j // 2) % X, j // 2, j // (2 * X)
    rows = coords.shape[0]
    run = Chain()

    second, first = jnp.where(k == 0, 3, 1), jnp.where(k == 0, 1, 3)
    order = jnp.stack([x, x ^ second, x ^ first, x ^ 2]).astype(jnp.int32)
    core = jnp.reshape(k, (1,)).astype(jnp.int32)

    def arrange(v):
        def body(ins, outs, _):
            for s in range(4):
                at = pl.multiple_of(ins[0][s] * Q, Q)
                outs[0][:, s * Q : (s + 1) * Q] = ins[1][:, pl.ds(at, Q)]

        return run("arrange", body, [like(v)], [order, v], [SM, VM])[0]

    unit, other = {}, {}
    f_far = lax.ppermute(forces, ("cfg", "mode"), FORCES)
    unit[0, 0] = arrange(coords)
    other[0, 0] = lax.ppermute(unit[0, 0], "mode", KSWAP)
    unit[0, 3] = lax.ppermute(unit[0, 0], "cfg", cfg_perm(0, 1))
    unit[0, 1] = lax.ppermute(unit[0, 0], "cfg", cfg_perm(0, -1))
    unit[1, 0] = lax.ppermute(unit[0, 0], "cfg", cfg_perm(1, 0))

    window = 6 * 128

    def slice_polar(ins, outs, scratch):
        at, scale, source = ins
        wide_t, narrow, sems = scratch
        moves = []
        for h in range(2):
            begin = pl.multiple_of(at[2 * h] * 128, 128)
            moves.append(pltpu.make_async_copy(source.at[:, pl.ds(begin, window)], narrow.at[h], sems.at[h]))
            moves[-1].start()
        for h in range(2):
            moves[h].wait()
            wide_t[...] = wide(narrow[h]).T * scale[...]
            skip = pl.multiple_of(at[2 * h + 1] * 8, 8)
            outs[h][...] = wide_t[pl.ds(skip, rows), :].astype(BF16)

    begins = [(2 * i + 1 - k) * rows, (2 * i + k) * rows]
    at = jnp.stack([v for b in begins for v in (b // 128, (b % 128) // 8)]).astype(jnp.int32)
    half = jax.ShapeDtypeStruct((rows, rows), BF16)
    px, po = run(
        "polar",
        slice_polar,
        [half, half],
        [at, curvature[None, :], polar],
        [SM, VM, HBM],
        scratch=[
            pltpu.VMEM((window, rows), F32),
            pltpu.VMEM((2, rows, window), BF16),
            pltpu.SemaphoreType.DMA((2,)),
        ],
        mib=54,
    )
    px = lax.ppermute(px, "mode", KSWAP)
    f_own = arrange(forces)

    def matmul1(chunk, f, flags):
        n = len(chunk)
        shapes = [jax.ShapeDtypeStruct((rows, w * n * Q), BF16) for w in (1, 1, 2)]

        def body(ins, outs, _):
            flag, a, b, fr = ins[:4]
            keep, s2, s1 = outs
            for u in range(n):
                h = jnp.dot(a[...], ins[4 + 2 * u][...], preferred_element_type=F32)
                h += jnp.dot(b[...], reorder(ins[5 + 2 * u][...]), preferred_element_type=F32)
                h += wide(fr[...]) * flag[u].astype(F32)
                h = h.astype(BF16)
                lo, hi = slice(u * Q, (u + 1) * Q), slice((n + u) * Q, (n + u + 1) * Q)
                keep[:, lo] = h[:, :Q]
                s2[:, lo] = h[:, Q : 2 * Q]
                s1[:, lo] = h[:, 2 * Q : 3 * Q]
                s1[:, hi] = h[:, 3 * Q :]

        args = [flags, po, px, f] + [v for u in chunk for v in (unit[u], other[u])]
        return run("product1", body, shapes, args, [SM] + [VM] * (len(args) - 1), mib=6 + 3 * n)

    def add(width, args, starts):
        def body(ins, outs, _):
            total = None
            for r, at in zip(ins, starts):
                v = wide(r[:, at : at + width])
                total = v if total is None else total + v
            outs[0][...] = total.astype(BF16)

        return run("add", body, [jax.ShapeDtypeStruct((rows, width), BF16)], args, [VM] * len(args))[0]

    def gate(args, pick=None):
        outs = [like(v) for v in args]
        scratch = []
        if pick:
            outs.append(like(args[pick[0]]))
            scratch = [pltpu.SemaphoreType.DMA]

        def body(ins, outs, sem):
            if pick:
                for c in range(2):

                    @pl.when(ins[0][0] == c)
                    def _():
                        move = pltpu.make_async_copy(ins[1 + pick[c]], outs[-1], sem[0])
                        move.start()
                        move.wait()

        aliases = {1 + a: a for a in range(len(args))}
        return run(
            "gate", body, outs, [core] + list(args), [SM] + [ANY] * len(args), [ANY] * len(outs), aliases, scratch
        )

    def join(a, b):
        w = a.shape[1]

        def body(ins, outs, _):
            outs[0][:, :w] = ins[0][...]
            outs[0][:, w:] = ins[1][...]

        return run("join", body, [jax.ShapeDtypeStruct((rows, 2 * w), BF16)], [a, b], [VM] * 2)[0]

    def matmul2(groups, acc, names, swap, dtype):
        begins = acc is None
        args = [] if begins else [acc]
        for chunk, r in groups:
            args += list(r) + [names[u] for u in chunk]

        def body(ins, outs, _):
            ins = list(ins)
            total = None if begins else ins.pop(0)[...]
            for chunk, _ in groups:
                n = len(chunk)
                pieces = [(r, h) for r in ins[:2] for h in range(2)]
                if swap:
                    pieces = [pieces[p] for p in (0, 2, 1, 3)]
                ins = ins[2:]
                for u in range(n):
                    ru = jnp.concatenate([r[:, (h * n + u) * Q : (h * n + u + 1) * Q] for r, h in pieces], axis=1)
                    t = lax.dot_general(
                        ins[u][...], ru, (((1,), (1,)), ((), ())), preferred_element_type=F32
                    )
                    total = t if total is None else total + t
                ins = ins[len(chunk) :]
            outs[0][...] = total.astype(dtype)

        return run("product2", body, [jax.ShapeDtypeStruct((rows, rows), dtype)], args, [VM] * len(args), mib=14)[0]

    last = len(CHUNKS) - 1
    keep, got1, half2, got2, part, got3, r0, r1, near_half, far_half = ({} for _ in range(10))
    own_sum = oth_sum = back = None
    f_all = None
    for step in STEPS:
        stage, c = step[0], int(step[1])
        chunk = CHUNKS[c]
        n = len(chunk)
        if stage == "M":
            if c == 0:
                flags = jnp.reshape(i == chip, (1,)).astype(jnp.int32)
                f = f_own
            else:
                if f_all is None:
                    f_all = arrange(f_far)
                f = f_all
                flags = jnp.stack(
                    [(((yh ^ dy) == yl) & ((2 * z + dz) % Z == x)).astype(jnp.int32) for dy, dz in chunk]
                )
            keep[c], half2[c], s1 = matmul1(chunk, f, flags)
            got1[c] = lax.ppermute(s1, "mode", FIRST)
        elif stage == "S":
            v = add(n * Q, [half2[c], got1[c]], [0, n * Q])
            got2[c] = lax.ppermute(v, "mode", SECOND)
        elif stage == "Y":
            part[c] = add(n * Q, [keep[c], got1[c], got2[c]], [0, 0, 0])
            got3[c] = lax.ppermute(part[c], "mode", YSWAP)
        elif stage == "R":
            r0[c] = add(n * Q, [part[c], got3[c]], [0, 0])
            r1[c] = lax.ppermute(r0[c], "mode", SECOND)
        elif stage == "F":
            near_half[c] = join(r0[c], r1[c])
            far_half[c] = lax.ppermute(near_half[c], "mode", FIRST)
        elif stage == "T":
            group = [(chunk, (near_half[c], far_half[c]))]
            oth_sum = matmul2(group, oth_sum, other, True, BF16 if c == last else F32)
            if c == last:
                back = lax.ppermute(oth_sum, "mode", KSWAP)
            own_sum = matmul2(group, own_sum, unit, False, F32)
        elif step == "G0":
            near = [(1, 0), (0, 3), (0, 1)]
            *vals, pick = gate([unit[u] for u in near], (1, 2))
            for u, v in zip(near, vals):
                unit[u] = v
                other[u] = lax.ppermute(v, "mode", KSWAP)
            unit[1, 3] = lax.ppermute(unit[1, 0], "cfg", cfg_perm(0, 1))
            unit[1, 1] = lax.ppermute(unit[1, 0], "cfg", cfg_perm(0, -1))
            unit[0, 2] = lax.ppermute(pick, ("cfg", "mode"), ONWARD)
        elif step == "G1":
            near = [(1, 3), (1, 1)]
            *vals, pick = gate([unit[u] for u in near], (0, 1))
            for u, v in zip(near, vals):
                unit[u] = v
                other[u] = lax.ppermute(v, "mode", KSWAP)
            unit[1, 2] = lax.ppermute(pick, ("cfg", "mode"), ONWARD)
        elif step == "G2":
            near = [(0, 2), (1, 2)]
            for u, v in zip(near, gate([unit[u] for u in near])):
                unit[u] = v
                other[u] = lax.ppermute(v, "mode", KSWAP)

    factor = weight[:, None] * (1.0 / math.sqrt(coords.shape[1] * lax.axis_size("cfg")))

    def finish(ins, outs, _):
        own, got = ins[2][...] * ins[1][...], wide(ins[3][...]) * ins[1][...]
        for c in range(2):

            @pl.when(ins[0][0] == c)
            def _():
                outs[0][:, :rows] = (own, got)[c]
                outs[0][:, rows:] = (got, own)[c]

    (out,) = run(
        "finish",
        finish,
        [jax.ShapeDtypeStruct((rows, 2 * rows), F32)],
        [core, factor, own_sum, back],
        [SM, VM, VM, VM],
        mib=12,
    )
    return out.T


def solution(mesh):
    placed = (P("mode", "cfg"), P("mode"), P("mode"), P("mode", None), P("mode", "cfg"))
    return jax.shard_map(
        on_device, mesh=mesh, in_specs=placed, out_specs=P("cfg", "mode"), check_vma=False
    )
```

```python
import math

import jax
import jax.numpy as jnp
from jax import lax
from jax.experimental import pallas as pl
from jax.experimental.pallas import tpu as pltpu
from jax.sharding import PartitionSpec as P

F32 = jnp.float32
BF16 = jnp.bfloat16
X, Z = 4, 4
Q = 128
CHUNKS = (((0, 0), (0, 3), (0, 1), (1, 0)), ((1, 3), (1, 1)), ((0, 2), (1, 2)))
STEPS = (
    "G0", "G3", "M0", "G1", "M1", "S0", "G2", "Y0", "M2",
    "S1", "S2", "Y1", "R0", "Y2", "F0", "R1", "F1", "R2",
    "F2", "T0", "T1", "T2",
)


def mode_perm(fn):
    out = []
    for j in range(16):
        yl, x, k = j // 8, (j // 2) % 4, j % 2
        a, b, c = fn(yl, x, k)
        out.append((j, (a * 4 + b) * 2 + c))
    return out


FIRST = mode_perm(lambda yl, x, k: (yl, x ^ (3 if k else 1), k))
SECOND = mode_perm(lambda yl, x, k: (yl, x ^ (1 if k else 3), k))
YSWAP = mode_perm(lambda yl, x, k: (1 - yl, x, k))
KSWAP = mode_perm(lambda yl, x, k: (yl, x, 1 - k))


def all_perm(fn):
    out = []
    for d in range(128):
        src = (d // 64, (d // 16) % 4, (d // 8) % 2, (d // 2) % 4, d % 2)
        a, b, c, e, k = fn(*src)
        out.append((d, (((a * 4 + b) * 2 + c) * 4 + e) * 2 + k))
    return out


def cfg_perm(dy, dz):
    return [(c, (c // 4 ^ dy) * 4 + (c % 4 + dz) % 4) for c in range(8)]


ONWARD = all_perm(lambda yh, z, yl, x, k: (yh, (z + (3 if k else 1)) % 4, yl, x, k))
FORCES = all_perm(lambda yh, z, yl, x, k: (yl, x, yh, (x + z) % 4, k))

VM = pl.BlockSpec(memory_space=pltpu.VMEM)
SM = pl.BlockSpec(memory_space=pltpu.SMEM)
ANY = pl.BlockSpec(memory_space=pl.ANY)
HBM = pl.BlockSpec(memory_space=pltpu.HBM)
TOKEN = jax.ShapeDtypeStruct((8, 128), F32)


class Chain:
    def __init__(self):
        self.token = None
        self.step = ""

    def __call__(self, name, body, outs, args, specs, out_specs=None, aliases=None, scratch=(), mib=4):
        given = self.token is not None
        n_in, n_out = len(args), len(outs)

        def kernel(*refs):
            ins = refs[:n_in]
            rest = refs[n_in + int(given) :]
            rest[n_out][...] = jnp.zeros((8, 128), F32)
            body(ins, rest[:n_out], rest[n_out + 1 :])

        res = pl.pallas_call(
            kernel,
            out_shape=list(outs) + [TOKEN],
            in_specs=list(specs) + ([ANY] if given else []),
            out_specs=(list(out_specs) if out_specs else [VM] * n_out) + [VM],
            input_output_aliases=aliases or {},
            scratch_shapes=list(scratch),
            compiler_params=pltpu.CompilerParams(vmem_limit_bytes=mib * 1024 * 1024),
            cost_estimate=pl.CostEstimate(flops=1000, bytes_accessed=1000, transcendentals=0),
            name=self.step + name,
        )(*args, *([self.token] if given else []))
        self.token = res[-1]
        return res[:-1]


def like(v):
    return jax.ShapeDtypeStruct(v.shape, v.dtype)


def wide(v):
    return v.astype(F32)


def reorder(v):
    return jnp.concatenate([v[:, :Q], v[:, 2 * Q : 3 * Q], v[:, Q : 2 * Q], v[:, 3 * Q :]], axis=1)


def on_device(coords, curvature, weight, polar, forces):
    rows = coords.shape[0]
    run = Chain()

    def place():
        i, j = lax.axis_index("cfg"), lax.axis_index("mode")
        return i, j // 2, j % 2

    def pieces():
        _, chip, k = place()
        x = chip % X
        return x, x ^ (3 - 2 * k), x ^ (1 + 2 * k), x ^ 2

    def columns(piece):
        return pl.ds(pl.multiple_of(piece * Q, Q), Q)

    def arrange(v):
        def body(ins, outs, _):
            for s, p in enumerate(pieces()):
                outs[0][:, s * Q : (s + 1) * Q] = ins[0][:, columns(p)]

        return run("arrange", body, [like(v)], [v], [VM])[0]

    unit, other = {}, {}
    f_far = lax.ppermute(forces, ("cfg", "mode"), FORCES)
    unit[0, 0] = arrange(coords)
    other[0, 0] = lax.ppermute(unit[0, 0], "mode", KSWAP)
    unit[0, 3] = lax.ppermute(unit[0, 0], "cfg", cfg_perm(0, 1))
    unit[0, 1] = lax.ppermute(unit[0, 0], "cfg", cfg_perm(0, -1))
    unit[1, 0] = lax.ppermute(unit[0, 0], "cfg", cfg_perm(1, 0))

    window = 6 * 128

    def slice_polar(ins, outs, scratch):
        scale, source = ins
        i, _, k = place()
        wide_t, narrow, sems = scratch
        moves = []
        begins = [(2 * i + 1 - k) * rows, (2 * i + k) * rows]
        for h in range(2):
            begin = pl.multiple_of(begins[h] // 128 * 128, 128)
            moves.append(pltpu.make_async_copy(source.at[:, pl.ds(begin, window)], narrow.at[h], sems.at[h]))
            moves[-1].start()
        for h in range(2):
            moves[h].wait()
            wide_t[...] = wide(narrow[h]).T * scale[...][None, :]
            skip = pl.multiple_of(begins[h] % 128, 8)
            outs[h][...] = wide_t[pl.ds(skip, rows), :].astype(BF16)

    half = jax.ShapeDtypeStruct((rows, rows), BF16)
    px, po = run(
        "polar",
        slice_polar,
        [half, half],
        [curvature, polar],
        [VM, HBM],
        scratch=[
            pltpu.VMEM((window, rows), F32),
            pltpu.VMEM((2, rows, window), BF16),
            pltpu.SemaphoreType.DMA((2,)),
        ],
        mib=52,
    )
    px = lax.ppermute(px, "mode", KSWAP)

    def matmul1(chunk, f):
        n = len(chunk)
        shapes = [jax.ShapeDtypeStruct((rows, w * n * Q), BF16) for w in (1, 1, 2)]

        def body(ins, outs, _):
            a, b, fr = ins[:3]
            keep, s2, s1 = outs
            i, chip, _ = place()
            for u, (dy, dz) in enumerate(chunk):
                yh, z, yl, x = i // Z ^ dy, i % Z, chip // X, chip % X
                here = (yh == yl) & ((2 * z + dz) % Z == x)
                flag = jnp.where(here, 1.0, 0.0)
                h = jnp.dot(a[...], ins[3 + 2 * u][...], preferred_element_type=F32)
                h += jnp.dot(b[...], reorder(ins[4 + 2 * u][...]), preferred_element_type=F32)
                part = [
                    (h[:, s * Q : (s + 1) * Q] + wide(fr[:, columns(p)]) * flag).astype(BF16)
                    for s, p in enumerate(pieces())
                ]
                lo, hi = slice(u * Q, (u + 1) * Q), slice((n + u) * Q, (n + u + 1) * Q)
                keep[:, lo] = part[0]
                s2[:, lo] = part[1]
                s1[:, lo] = part[2]
                s1[:, hi] = part[3]

        args = [po, px, f] + [v for u in chunk for v in (unit[u], other[u])]
        return run("product1", body, shapes, args, [VM] * len(args), mib=6 + 3 * n)

    def add(width, args, starts):
        def body(ins, outs, _):
            total = None
            for r, at in zip(ins, starts):
                v = wide(r[:, at : at + width])
                total = v if total is None else total + v
            outs[0][...] = total.astype(BF16)

        return run("add", body, [jax.ShapeDtypeStruct((rows, width), BF16)], args, [VM] * len(args))[0]

    def gate(args, pick=None):
        outs = [like(v) for v in args]
        scratch = []
        if pick:
            outs.append(like(args[pick[0]]))
            scratch = [pltpu.SemaphoreType.DMA]

        def body(ins, outs, sem):
            if pick:
                for c in range(2):

                    @pl.when(place()[2] == c)
                    def _():
                        move = pltpu.make_async_copy(ins[pick[c]], outs[-1], sem[0])
                        move.start()
                        move.wait()

        aliases = {a: a for a in range(len(args))}
        return run("gate", body, outs, list(args), [ANY] * len(args), [ANY] * len(outs), aliases, scratch)

    def join(a, b):
        w = a.shape[1]

        def body(ins, outs, _):
            outs[0][:, :w] = ins[0][...]
            outs[0][:, w:] = ins[1][...]

        return run("join", body, [jax.ShapeDtypeStruct((rows, 2 * w), BF16)], [a, b], [VM] * 2)[0]

    def matmul2(groups, acc, names, swap, dtype):
        begins = acc is None
        args = [] if begins else [acc]
        for chunk, r in groups:
            args += list(r) + [names[u] for u in chunk]

        def body(ins, outs, _):
            ins = list(ins)
            total = None if begins else ins.pop(0)[...]
            for chunk, _ in groups:
                n = len(chunk)
                pieces = [(r, h) for r in ins[:2] for h in range(2)]
                if swap:
                    pieces = [pieces[p] for p in (0, 2, 1, 3)]
                ins = ins[2:]
                for u in range(n):
                    ru = jnp.concatenate([r[:, (h * n + u) * Q : (h * n + u + 1) * Q] for r, h in pieces], axis=1)
                    t = lax.dot_general(
                        ins[u][...], ru, (((1,), (1,)), ((), ())), preferred_element_type=F32
                    )
                    total = t if total is None else total + t
                ins = ins[len(chunk) :]
            outs[0][...] = total.astype(dtype)

        return run("product2", body, [jax.ShapeDtypeStruct((rows, rows), dtype)], args, [VM] * len(args), mib=14)[0]

    last = len(CHUNKS) - 1
    keep, got1, half2, got2, part, got3, r0, r1, near_half, far_half = ({} for _ in range(10))
    own_sum = oth_sum = back = None
    done = 0
    for step in STEPS:
        run.step = step.lower() + "_"
        stage, c = step[0], int(step[1])
        chunk = CHUNKS[c] if stage != "G" else ()
        n = len(chunk)
        if stage == "M":
            keep[c], half2[c], s1 = matmul1(chunk, f_far)
            got1[c] = lax.ppermute(s1, "mode", FIRST)
        elif stage == "S":
            v = add(n * Q, [half2[c], got1[c]], [0, n * Q])
            got2[c] = lax.ppermute(v, "mode", SECOND)
        elif stage == "Y":
            part[c] = add(n * Q, [keep[c], got1[c], got2[c]], [0, 0, 0])
            got3[c] = lax.ppermute(part[c], "mode", YSWAP)
        elif stage == "R":
            r0[c] = add(n * Q, [part[c], got3[c]], [0, 0])
            r1[c] = lax.ppermute(r0[c], "mode", SECOND)
        elif stage == "F":
            near_half[c] = join(r0[c], r1[c])
            far_half[c] = lax.ppermute(near_half[c], "mode", FIRST)
        elif stage == "T":
            group = [(CHUNKS[d], (near_half[d], far_half[d])) for d in range(done, c + 1)]
            done = c + 1
            oth_sum = matmul2(group, oth_sum, other, True, BF16 if c == last else F32)
            if c == last:
                back = lax.ppermute(oth_sum, "mode", KSWAP)
            own_sum = matmul2(group, own_sum, unit, False, F32)
        elif step == "G0":
            near = [(1, 0), (0, 3), (0, 1)]
            *vals, pick = gate([unit[u] for u in near], (1, 2))
            for u, v in zip(near, vals):
                unit[u] = v
                other[u] = lax.ppermute(v, "mode", KSWAP)
            unit[1, 3] = lax.ppermute(unit[1, 0], "cfg", cfg_perm(0, 1))
            unit[1, 1] = lax.ppermute(unit[1, 0], "cfg", cfg_perm(0, -1))
            unit[0, 2] = lax.ppermute(pick, ("cfg", "mode"), ONWARD)
        elif step == "G1":
            near = [(1, 3), (1, 1)]
            *vals, pick = gate([unit[u] for u in near], (0, 1))
            for u, v in zip(near, vals):
                unit[u] = v
                other[u] = lax.ppermute(v, "mode", KSWAP)
            unit[1, 2] = lax.ppermute(pick, ("cfg", "mode"), ONWARD)
        elif step == "G3":
            (f_far,) = gate([f_far])
        elif step == "G2":
            near = [(0, 2), (1, 2)]
            for u, v in zip(near, gate([unit[u] for u in near])):
                unit[u] = v
                other[u] = lax.ppermute(v, "mode", KSWAP)

    factor = weight[:, None] * (1.0 / math.sqrt(coords.shape[1] * lax.axis_size("cfg")))

    def finish(ins, outs, _):
        own, got = ins[1][...] * ins[0][...], wide(ins[2][...]) * ins[0][...]
        for c in range(2):

            @pl.when(place()[2] == c)
            def _():
                outs[0][:, :rows] = (own, got)[c]
                outs[0][:, rows:] = (got, own)[c]


    shape = jax.ShapeDtypeStruct((rows, 2 * rows), F32)
    (out,) = run("finish", finish, [shape], [factor, own_sum, back], [VM, VM, VM], mib=12)
    return out.T


def solution(mesh):
    placed = (P("mode", "cfg"), P("mode"), P("mode"), P("mode", None), P("mode", "cfg"))
    return jax.shard_map(
        on_device, mesh=mesh, in_specs=placed, out_specs=P("cfg", "mode"), check_vma=False
    )
```

```python
import math

import jax
import jax.numpy as jnp
from jax import lax
from jax.experimental import pallas as pl
from jax.experimental.pallas import tpu as pltpu
from jax.sharding import PartitionSpec as P

F32 = jnp.float32
BF16 = jnp.bfloat16
X, Z = 4, 4
Q = 128
CHUNKS = (((0, 0), (0, 3), (0, 1), (1, 0)), ((1, 3), (1, 1)), ((0, 2), (1, 2)))
FINISH = 3
STEPS = (
    "G0", "G3", "M0", "G1", "M1", "S0", "G2", "Y0", "M2",
    "S1", "Y1", "R0", "S2", "R1", "F0", "Y2", "R2", "F1",
    "F2", "N2", "T0", "T1", "T2",
)


def mode_perm(fn):
    out = []
    for j in range(16):
        yl, x, k = j // 8, (j // 2) % 4, j % 2
        a, b, c = fn(yl, x, k)
        out.append((j, (a * 4 + b) * 2 + c))
    return out


FIRST = mode_perm(lambda yl, x, k: (yl, x ^ (3 if k else 1), k))
SECOND = mode_perm(lambda yl, x, k: (yl, x ^ (1 if k else 3), k))
YSWAP = mode_perm(lambda yl, x, k: (1 - yl, x, k))
KSWAP = mode_perm(lambda yl, x, k: (yl, x, 1 - k))


def all_perm(fn):
    out = []
    for d in range(128):
        src = (d // 64, (d // 16) % 4, (d // 8) % 2, (d // 2) % 4, d % 2)
        a, b, c, e, k = fn(*src)
        out.append((d, (((a * 4 + b) * 2 + c) * 4 + e) * 2 + k))
    return out


def cfg_perm(dy, dz):
    return [(c, (c // 4 ^ dy) * 4 + (c % 4 + dz) % 4) for c in range(8)]


ONWARD = all_perm(lambda yh, z, yl, x, k: (yh, (z + (3 if k else 1)) % 4, yl, x, k))
FORCES = all_perm(lambda yh, z, yl, x, k: (yl, x, yh, (x + z) % 4, k))

VM = pl.BlockSpec(memory_space=pltpu.VMEM)
SM = pl.BlockSpec(memory_space=pltpu.SMEM)
ANY = pl.BlockSpec(memory_space=pl.ANY)
HBM = pl.BlockSpec(memory_space=pltpu.HBM)
TOKEN = jax.ShapeDtypeStruct((8, 128), F32)


class Chain:
    def __init__(self):
        self.token = None
        self.step = ""

    def __call__(self, name, body, outs, args, specs, out_specs=None, aliases=None, scratch=(), mib=4):
        given = self.token is not None
        n_in, n_out = len(args), len(outs)

        def kernel(*refs):
            ins = refs[:n_in]
            rest = refs[n_in + int(given) :]
            rest[n_out][...] = jnp.zeros((8, 128), F32)
            body(ins, rest[:n_out], rest[n_out + 1 :])

        res = pl.pallas_call(
            kernel,
            out_shape=list(outs) + [TOKEN],
            in_specs=list(specs) + ([ANY] if given else []),
            out_specs=(list(out_specs) if out_specs else [VM] * n_out) + [VM],
            input_output_aliases=aliases or {},
            scratch_shapes=list(scratch),
            compiler_params=pltpu.CompilerParams(vmem_limit_bytes=mib * 1024 * 1024),
            cost_estimate=pl.CostEstimate(flops=1000, bytes_accessed=1000, transcendentals=0),
            name=self.step + name,
        )(*args, *([self.token] if given else []))
        self.token = res[-1]
        return res[:-1]


def like(v):
    return jax.ShapeDtypeStruct(v.shape, v.dtype)


def wide(v):
    return v.astype(F32)


def reorder(v):
    return jnp.concatenate([v[:, :Q], v[:, 2 * Q : 3 * Q], v[:, Q : 2 * Q], v[:, 3 * Q :]], axis=1)


def on_device(coords, curvature, weight, polar, forces):
    rows = coords.shape[0]
    run = Chain()

    def place():
        i, j = lax.axis_index("cfg"), lax.axis_index("mode")
        return i, j // 2, j % 2

    def pieces():
        _, chip, k = place()
        x = chip % X
        return x, x ^ (3 - 2 * k), x ^ (1 + 2 * k), x ^ 2

    def columns(piece):
        return pl.ds(pl.multiple_of(piece * Q, Q), Q)

    def arrange(v):
        def body(ins, outs, _):
            for s, p in enumerate(pieces()):
                outs[0][:, s * Q : (s + 1) * Q] = ins[0][:, columns(p)]

        return run("arrange", body, [like(v)], [v], [VM])[0]

    unit, other = {}, {}
    f_far = lax.ppermute(forces, ("cfg", "mode"), FORCES)
    unit[0, 0] = arrange(coords)
    other[0, 0] = lax.ppermute(unit[0, 0], "mode", KSWAP)
    unit[0, 3] = lax.ppermute(unit[0, 0], "cfg", cfg_perm(0, 1))
    unit[0, 1] = lax.ppermute(unit[0, 0], "cfg", cfg_perm(0, -1))
    unit[1, 0] = lax.ppermute(unit[0, 0], "cfg", cfg_perm(1, 0))

    window = 6 * 128

    def slice_polar(ins, outs, scratch):
        scale, source = ins
        i, _, k = place()
        wide_t, narrow, sems = scratch
        moves = []
        begins = [(2 * i + 1 - k) * rows, (2 * i + k) * rows]
        for h in range(2):
            begin = pl.multiple_of(begins[h] // 128 * 128, 128)
            moves.append(pltpu.make_async_copy(source.at[:, pl.ds(begin, window)], narrow.at[h], sems.at[h]))
            moves[-1].start()
        for h in range(2):
            moves[h].wait()
            wide_t[...] = wide(narrow[h]).T * scale[...][None, :]
            skip = pl.multiple_of(begins[h] % 128, 8)
            outs[h][...] = wide_t[pl.ds(skip, rows), :].astype(BF16)

    half = jax.ShapeDtypeStruct((rows, rows), BF16)
    px, po = run(
        "polar",
        slice_polar,
        [half, half],
        [curvature, polar],
        [VM, HBM],
        scratch=[
            pltpu.VMEM((window, rows), F32),
            pltpu.VMEM((2, rows, window), BF16),
            pltpu.SemaphoreType.DMA((2,)),
        ],
        mib=52,
    )
    px = lax.ppermute(px, "mode", KSWAP)

    def matmul1(chunk, f, early):
        n = len(chunk)
        shapes = [jax.ShapeDtypeStruct((rows, w * n * Q), BF16) for w in (1, 1, 2)]

        def body(ins, outs, _):
            a, b, fr = ins[:3]
            keep, s2, s1 = outs
            i, chip, _ = place()
            for u, (dy, dz) in enumerate(chunk):
                yh, z, yl, x = i // Z ^ dy, i % Z, chip // X, chip % X
                here = (i == chip) if early else (yh == yl) & ((2 * z + dz) % Z == x)
                flag = jnp.where(here, 1.0, 0.0)
                h = jnp.dot(a[...], ins[3 + 2 * u][...], preferred_element_type=F32)
                h += jnp.dot(b[...], reorder(ins[4 + 2 * u][...]), preferred_element_type=F32)
                part = [
                    (h[:, s * Q : (s + 1) * Q] + wide(fr[:, columns(p)]) * flag).astype(BF16)
                    for s, p in enumerate(pieces())
                ]
                lo, hi = slice(u * Q, (u + 1) * Q), slice((n + u) * Q, (n + u + 1) * Q)
                keep[:, lo] = part[0]
                s2[:, lo] = part[1]
                s1[:, lo] = part[2]
                s1[:, hi] = part[3]

        args = [po, px, f] + [v for u in chunk for v in (unit[u], other[u])]
        return run("product1", body, shapes, args, [VM] * len(args), mib=6 + 3 * n)

    def add(products, which, far, more=()):
        args = [v for p in products for v in (p[which], p[3])] + list(more)
        sizes = [p[which].shape[1] for p in products]

        def body(ins, outs, _):
            at = 0
            for q, w in enumerate(sizes):
                got = ins[2 * q + 1]
                total = wide(ins[2 * q][...]) + wide(got[:, w:] if far else got[:, :w])
                for r in ins[2 * len(sizes) :]:
                    total += wide(r[:, at : at + w])
                outs[0][:, at : at + w] = total.astype(BF16)
                at += w

        return run("add", body, [jax.ShapeDtypeStruct((rows, sum(sizes)), BF16)], args, [VM] * len(args), mib=6)[0]

    def add2(a, b):
        def body(ins, outs, _):
            outs[0][...] = (wide(ins[0][...]) + wide(ins[1][...])).astype(BF16)

        return run("add", body, [like(a)], [a, b], [VM] * 2)[0]

    def gate(args, pick=None):
        outs = [like(v) for v in args]
        scratch = []
        if pick:
            outs.append(like(args[pick[0]]))
            scratch = [pltpu.SemaphoreType.DMA]

        def body(ins, outs, sem):
            if pick:
                for c in range(2):

                    @pl.when(place()[2] == c)
                    def _():
                        move = pltpu.make_async_copy(ins[pick[c]], outs[-1], sem[0])
                        move.start()
                        move.wait()

        aliases = {a: a for a in range(len(args))}
        return run("gate", body, outs, list(args), [ANY] * len(args), [ANY] * len(outs), aliases, scratch)

    def join(a, b):
        w = a.shape[1]

        def body(ins, outs, _):
            outs[0][:, :w] = ins[0][...]
            outs[0][:, w:] = ins[1][...]

        return run("join", body, [jax.ShapeDtypeStruct((rows, 2 * w), BF16)], [a, b], [VM] * 2)[0]

    def matmul2(groups, acc, names, swap, dtype, far):
        begins = acc is None
        args = [] if begins else [acc]
        for chunk, r in groups:
            args += [r] + [names[u] for u in chunk]
        places = [(0, 2, 1, 3)[s] if swap else s for s in ((2, 3) if far else (0, 1))]

        def body(ins, outs, _):
            ins = list(ins)
            total = None if begins else ins.pop(0)[...]
            for chunk, _ in groups:
                n, r, ins = len(chunk), ins[0], ins[1:]
                for u in range(n):
                    ru = jnp.concatenate([r[:, (h * n + u) * Q : (h * n + u + 1) * Q] for h in range(2)], axis=1)
                    cu = jnp.concatenate([ins[u][:, p * Q : (p + 1) * Q] for p in places], axis=1)
                    t = lax.dot_general(cu, ru, (((1,), (1,)), ((), ())), preferred_element_type=F32)
                    total = t if total is None else total + t
                ins = ins[n:]
            outs[0][...] = total.astype(dtype)

        shape = jax.ShapeDtypeStruct((rows, rows), dtype)
        return run("product2", body, [shape], args, [VM] * len(args), mib=6 + 2 * sum(len(g[0]) for g in groups))[0]

    last = len(CHUNKS) - 1
    products = [[] for _ in CHUNKS]
    got2, part3, got3, r0, r1, near_half, far_half = ({} for _ in range(7))
    own_sum = oth_sum = back = None
    begun = done = 0
    for step in STEPS:
        run.step = step.lower() + "_"
        stage, c = step[0], int(step[1])
        chunk = CHUNKS[c] if stage != "G" else ()
        if stage in "AM":
            early = stage == "A"
            part = chunk[:1] if early else chunk[len(products[c]) :]
            got = matmul1(part, forces if early else f_far, early)
            products[c].append((*got, lax.ppermute(got[2], "mode", FIRST)))
        elif stage == "S":
            v = add(products[c], 1, True)
            got2[c] = lax.ppermute(v, "mode", SECOND)
        elif stage == "Y":
            part3[c] = add(products[c], 0, False, [got2[c]])
            got3[c] = lax.ppermute(part3[c], "mode", YSWAP)
        elif stage == "R":
            r0[c] = add2(part3[c], got3[c])
            r1[c] = lax.ppermute(r0[c], "mode", SECOND)
        elif stage == "F":
            near_half[c] = join(r0[c], r1[c])
            far_half[c] = lax.ppermute(near_half[c], "mode", FIRST)
        elif stage == "N":
            group = [(CHUNKS[d], near_half[d]) for d in range(begun, c + 1)]
            begun = c + 1
            oth_sum = matmul2(group, oth_sum, other, True, F32, False)
            own_sum = matmul2(group, own_sum, unit, False, F32, False)
        elif stage == "T":
            group = [(CHUNKS[d], far_half[d]) for d in range(done, c + 1)]
            done = c + 1
            oth_sum = matmul2(group, oth_sum, other, True, BF16 if c == last else F32, True)
            if c == last:
                back = lax.ppermute(oth_sum, "mode", KSWAP)
            own_sum = matmul2(group, own_sum, unit, False, F32, True)
        elif step == "G0":
            near = [(1, 0), (0, 3), (0, 1)]
            *vals, pick = gate([unit[u] for u in near], (1, 2))
            for u, v in zip(near, vals):
                unit[u] = v
                other[u] = lax.ppermute(v, "mode", KSWAP)
            unit[1, 3] = lax.ppermute(unit[1, 0], "cfg", cfg_perm(0, 1))
            unit[1, 1] = lax.ppermute(unit[1, 0], "cfg", cfg_perm(0, -1))
            unit[0, 2] = lax.ppermute(pick, ("cfg", "mode"), ONWARD)
        elif step == "G1":
            near = [(1, 3), (1, 1)]
            *vals, pick = gate([unit[u] for u in near], (0, 1))
            for u, v in zip(near, vals):
                unit[u] = v
                other[u] = lax.ppermute(v, "mode", KSWAP)
            unit[1, 2] = lax.ppermute(pick, ("cfg", "mode"), ONWARD)
        elif step == "G3":
            (f_far,) = gate([f_far])
        elif step == "G2":
            near = [(0, 2), (1, 2)]
            for u, v in zip(near, gate([unit[u] for u in near])):
                unit[u] = v
                other[u] = lax.ppermute(v, "mode", KSWAP)

    factor = weight[:, None] * (1.0 / math.sqrt(coords.shape[1] * lax.axis_size("cfg")))

    def finish(ins, outs, _):
        own, got = ins[1][...] * ins[0][...], wide(ins[2][...]) * ins[0][...]
        for c in range(2):

            @pl.when(place()[2] == c)
            def _():
                outs[0][:, :rows] = (own, got)[c]
                outs[0][:, rows:] = (got, own)[c]

    cut = FINISH if rows % (8 * FINISH) == 0 else 1
    shape = jax.ShapeDtypeStruct((rows, 2 * rows), F32)
    out = pl.pallas_call(
        lambda *refs: finish(refs[:3], refs[3:], ()),
        out_shape=shape,
        grid=(cut,),
        in_specs=[pl.BlockSpec((rows // cut, w), lambda t: (t, 0)) for w in (1, rows, rows)],
        out_specs=pl.BlockSpec((rows // cut, 2 * rows), lambda t: (t, 0)),
        compiler_params=pltpu.CompilerParams(vmem_limit_bytes=16 * 1024 * 1024),
        name="finish",
    )(factor, own_sum, back)
    return out.T


def solution(mesh):
    placed = (P("mode", "cfg"), P("mode"), P("mode"), P("mode", None), P("mode", "cfg"))
    return jax.shard_map(
        on_device, mesh=mesh, in_specs=placed, out_specs=P("cfg", "mode"), check_vma=False
    )
```

```python
import math

import jax
import jax.numpy as jnp
from jax import lax
from jax.experimental import pallas as pl
from jax.experimental.pallas import tpu as pltpu
from jax.sharding import PartitionSpec as P

F32 = jnp.float32
BF16 = jnp.bfloat16
X, Z = 4, 4
Q = 128
CHUNKS = (((0, 0), (0, 3), (0, 1), (1, 0)), ((1, 3), (1, 1)), ((0, 2), (1, 2)))
SHARED = (0,)
FINISH = 3
STEPS = (
    "G0", "G3", "M0", "G1", "M1", "S0", "G2", "Y0", "M2",
    "S1", "Y1", "R0", "S2", "R1", "F0", "Y2", "R2", "W0",
    "F1", "F2", "N2", "T1", "T0", "T2",
)


def mode_perm(fn):
    out = []
    for j in range(16):
        yl, x, k = j // 8, (j // 2) % 4, j % 2
        a, b, c = fn(yl, x, k)
        out.append((j, (a * 4 + b) * 2 + c))
    return out


FIRST = mode_perm(lambda yl, x, k: (yl, x ^ (3 if k else 1), k))
SECOND = mode_perm(lambda yl, x, k: (yl, x ^ (1 if k else 3), k))
YSWAP = mode_perm(lambda yl, x, k: (1 - yl, x, k))
KSWAP = mode_perm(lambda yl, x, k: (yl, x, 1 - k))


def all_perm(fn):
    out = []
    for d in range(128):
        src = (d // 64, (d // 16) % 4, (d // 8) % 2, (d // 2) % 4, d % 2)
        a, b, c, e, k = fn(*src)
        out.append((d, (((a * 4 + b) * 2 + c) * 4 + e) * 2 + k))
    return out


def cfg_perm(dy, dz):
    return [(c, (c // 4 ^ dy) * 4 + (c % 4 + dz) % 4) for c in range(8)]


ONWARD = all_perm(lambda yh, z, yl, x, k: (yh, (z + (3 if k else 1)) % 4, yl, x, k))
FORCES = all_perm(lambda yh, z, yl, x, k: (yl, x, yh, (x + z) % 4, k))

VM = pl.BlockSpec(memory_space=pltpu.VMEM)
SM = pl.BlockSpec(memory_space=pltpu.SMEM)
ANY = pl.BlockSpec(memory_space=pl.ANY)
HBM = pl.BlockSpec(memory_space=pltpu.HBM)
TOKEN = jax.ShapeDtypeStruct((8, 128), F32)


class Chain:
    def __init__(self):
        self.token = None
        self.step = ""

    def __call__(self, name, body, outs, args, specs, out_specs=None, aliases=None, scratch=(), mib=4):
        given = self.token is not None
        n_in, n_out = len(args), len(outs)

        def kernel(*refs):
            ins = refs[:n_in]
            rest = refs[n_in + int(given) :]
            rest[n_out][...] = jnp.zeros((8, 128), F32)
            body(ins, rest[:n_out], rest[n_out + 1 :])

        res = pl.pallas_call(
            kernel,
            out_shape=list(outs) + [TOKEN],
            in_specs=list(specs) + ([ANY] if given else []),
            out_specs=(list(out_specs) if out_specs else [VM] * n_out) + [VM],
            input_output_aliases=aliases or {},
            scratch_shapes=list(scratch),
            compiler_params=pltpu.CompilerParams(vmem_limit_bytes=mib * 1024 * 1024),
            cost_estimate=pl.CostEstimate(flops=1000, bytes_accessed=1000, transcendentals=0),
            name=self.step + name,
        )(*args, *([self.token] if given else []))
        self.token = res[-1]
        return res[:-1]


def like(v):
    return jax.ShapeDtypeStruct(v.shape, v.dtype)


def wide(v):
    return v.astype(F32)


def reorder(v):
    return jnp.concatenate([v[:, :Q], v[:, 2 * Q : 3 * Q], v[:, Q : 2 * Q], v[:, 3 * Q :]], axis=1)


def on_device(coords, curvature, weight, polar, forces):
    rows = coords.shape[0]
    run = Chain()

    def place():
        i, j = lax.axis_index("cfg"), lax.axis_index("mode")
        return i, j // 2, j % 2

    def pieces():
        _, chip, k = place()
        x = chip % X
        return x, x ^ (3 - 2 * k), x ^ (1 + 2 * k), x ^ 2

    def columns(piece):
        return pl.ds(pl.multiple_of(piece * Q, Q), Q)

    def arrange(v):
        def body(ins, outs, _):
            for s, p in enumerate(pieces()):
                outs[0][:, s * Q : (s + 1) * Q] = ins[0][:, columns(p)]

        return run("arrange", body, [like(v)], [v], [VM])[0]

    unit, other = {}, {}
    f_far = lax.ppermute(forces, ("cfg", "mode"), FORCES)
    unit[0, 0] = arrange(coords)
    other[0, 0] = lax.ppermute(unit[0, 0], "mode", KSWAP)
    unit[0, 3] = lax.ppermute(unit[0, 0], "cfg", cfg_perm(0, 1))
    unit[0, 1] = lax.ppermute(unit[0, 0], "cfg", cfg_perm(0, -1))
    unit[1, 0] = lax.ppermute(unit[0, 0], "cfg", cfg_perm(1, 0))

    window = 6 * 128

    def slice_polar(ins, outs, scratch):
        scale, source = ins
        i, _, k = place()
        wide_t, narrow, sems = scratch
        moves = []
        begins = [(2 * i + 1 - k) * rows, (2 * i + k) * rows]
        for h in range(2):
            begin = pl.multiple_of(begins[h] // 128 * 128, 128)
            moves.append(pltpu.make_async_copy(source.at[:, pl.ds(begin, window)], narrow.at[h], sems.at[h]))
            moves[-1].start()
        for h in range(2):
            moves[h].wait()
            wide_t[...] = wide(narrow[h]).T * scale[...][None, :]
            skip = pl.multiple_of(begins[h] % 128, 8)
            outs[h][...] = wide_t[pl.ds(skip, rows), :].astype(BF16)

    half = jax.ShapeDtypeStruct((rows, rows), BF16)
    px, po = run(
        "polar",
        slice_polar,
        [half, half],
        [curvature, polar],
        [VM, HBM],
        scratch=[
            pltpu.VMEM((window, rows), F32),
            pltpu.VMEM((2, rows, window), BF16),
            pltpu.SemaphoreType.DMA((2,)),
        ],
        mib=52,
    )
    px = lax.ppermute(px, "mode", KSWAP)

    def matmul1(chunk, f, early):
        n = len(chunk)
        shapes = [jax.ShapeDtypeStruct((rows, w * n * Q), BF16) for w in (1, 1, 2)]

        def body(ins, outs, _):
            a, b, fr = ins[:3]
            keep, s2, s1 = outs
            i, chip, _ = place()
            for u, (dy, dz) in enumerate(chunk):
                yh, z, yl, x = i // Z ^ dy, i % Z, chip // X, chip % X
                here = (i == chip) if early else (yh == yl) & ((2 * z + dz) % Z == x)
                flag = jnp.where(here, 1.0, 0.0)
                h = jnp.dot(a[...], ins[3 + 2 * u][...], preferred_element_type=F32)
                h += jnp.dot(b[...], reorder(ins[4 + 2 * u][...]), preferred_element_type=F32)
                part = [
                    (h[:, s * Q : (s + 1) * Q] + wide(fr[:, columns(p)]) * flag).astype(BF16)
                    for s, p in enumerate(pieces())
                ]
                lo, hi = slice(u * Q, (u + 1) * Q), slice((n + u) * Q, (n + u + 1) * Q)
                keep[:, lo] = part[0]
                s2[:, lo] = part[1]
                s1[:, lo] = part[2]
                s1[:, hi] = part[3]

        args = [po, px, f] + [v for u in chunk for v in (unit[u], other[u])]
        return run("product1", body, shapes, args, [VM] * len(args), mib=6 + 3 * n)

    def add(products, which, far, more=()):
        args = [v for p in products for v in (p[which], p[3])] + list(more)
        sizes = [p[which].shape[1] for p in products]

        def body(ins, outs, _):
            at = 0
            for q, w in enumerate(sizes):
                got = ins[2 * q + 1]
                total = wide(ins[2 * q][...]) + wide(got[:, w:] if far else got[:, :w])
                for r in ins[2 * len(sizes) :]:
                    total += wide(r[:, at : at + w])
                outs[0][:, at : at + w] = total.astype(BF16)
                at += w

        return run("add", body, [jax.ShapeDtypeStruct((rows, sum(sizes)), BF16)], args, [VM] * len(args), mib=6)[0]

    def add2(a, b):
        def body(ins, outs, _):
            outs[0][...] = (wide(ins[0][...]) + wide(ins[1][...])).astype(BF16)

        return run("add", body, [like(a)], [a, b], [VM] * 2)[0]

    def gate(args, pick=None):
        outs = [like(v) for v in args]
        scratch = []
        if pick:
            outs.append(like(args[pick[0]]))
            scratch = [pltpu.SemaphoreType.DMA]

        def body(ins, outs, sem):
            if pick:
                for c in range(2):

                    @pl.when(place()[2] == c)
                    def _():
                        move = pltpu.make_async_copy(ins[pick[c]], outs[-1], sem[0])
                        move.start()
                        move.wait()

        aliases = {a: a for a in range(len(args))}
        return run("gate", body, outs, list(args), [ANY] * len(args), [ANY] * len(outs), aliases, scratch)

    def join(a, b):
        w = a.shape[1]

        def body(ins, outs, _):
            outs[0][:, :w] = ins[0][...]
            outs[0][:, w:] = ins[1][...]

        return run("join", body, [jax.ShapeDtypeStruct((rows, 2 * w), BF16)], [a, b], [VM] * 2)[0]

    def is_low():
        return place()[1] // X == 0

    def join_and_pick(a, b):
        w = a.shape[1]

        def body(ins, outs, _):
            outs[0][:, :w] = ins[0][...]
            outs[0][:, w:] = ins[1][...]
            for side in range(2):

                @pl.when(is_low() == (side == 0))
                def _():
                    outs[1][...] = ins[side][...]

        shapes = [jax.ShapeDtypeStruct((rows, 2 * w), BF16), like(a)]
        return run("join", body, shapes, [a, b], [VM] * 2, mib=6)

    def merge(mine, across):
        w = mine.shape[1]

        def body(ins, outs, _):
            for side in range(2):

                @pl.when(is_low() == (side == 0))
                def _():
                    outs[0][:, :w] = ins[side][...]
                    outs[0][:, w:] = ins[1 - side][...]

        return run("merge", body, [jax.ShapeDtypeStruct((rows, 2 * w), BF16)], [mine, across], [VM] * 2, mib=6)[0]

    def matmul2(groups, acc, names, swap, dtype, far):
        begins = acc is None
        args = [] if begins else [acc]
        for chunk, r in groups:
            args += [r] + [names[u] for u in chunk]
        places = [(0, 2, 1, 3)[s] if swap else s for s in ((2, 3) if far else (0, 1))]

        def body(ins, outs, _):
            ins = list(ins)
            total = None if begins else ins.pop(0)[...]
            for chunk, _ in groups:
                n, r, ins = len(chunk), ins[0], ins[1:]
                for u in range(n):
                    ru = jnp.concatenate([r[:, (h * n + u) * Q : (h * n + u + 1) * Q] for h in range(2)], axis=1)
                    cu = jnp.concatenate([ins[u][:, p * Q : (p + 1) * Q] for p in places], axis=1)
                    t = lax.dot_general(cu, ru, (((1,), (1,)), ((), ())), preferred_element_type=F32)
                    total = t if total is None else total + t
                ins = ins[n:]
            outs[0][...] = total.astype(dtype)

        shape = jax.ShapeDtypeStruct((rows, rows), dtype)
        return run("product2", body, [shape], args, [VM] * len(args), mib=6 + 2 * sum(len(g[0]) for g in groups))[0]

    last = len(CHUNKS) - 1
    products = [[] for _ in CHUNKS]
    got2, part3, got3, r0, r1, near_half, far_half = ({} for _ in range(7))
    share, across = {}, {}
    own_sum = oth_sum = back = None
    begun = 0
    for step in STEPS:
        run.step = step.lower() + "_"
        stage, c = step[0], int(step[1])
        chunk = CHUNKS[c] if stage != "G" else ()
        if stage in "AM":
            early = stage == "A"
            part = chunk[:1] if early else chunk[len(products[c]) :]
            got = matmul1(part, forces if early else f_far, early)
            products[c].append((*got, lax.ppermute(got[2], "mode", FIRST)))
        elif stage == "S":
            v = add(products[c], 1, True)
            got2[c] = lax.ppermute(v, "mode", SECOND)
        elif stage == "Y":
            part3[c] = add(products[c], 0, False, [got2[c]])
            got3[c] = lax.ppermute(part3[c], "mode", YSWAP)
        elif stage == "R":
            r0[c] = add2(part3[c], got3[c])
            r1[c] = lax.ppermute(r0[c], "mode", SECOND)
        elif stage == "F":
            if c in SHARED:
                near_half[c], chosen = join_and_pick(r0[c], r1[c])
                share[c] = lax.ppermute(chosen, "mode", FIRST)
            else:
                near_half[c] = join(r0[c], r1[c])
                far_half[c] = lax.ppermute(near_half[c], "mode", FIRST)
        elif stage == "W":
            (share[c],) = gate([share[c]])
            across[c] = lax.ppermute(share[c], "mode", YSWAP)
        elif stage == "N":
            group = [(CHUNKS[d], near_half[d]) for d in range(begun, c + 1)]
            begun = c + 1
            oth_sum = matmul2(group, oth_sum, other, True, F32, False)
            own_sum = matmul2(group, own_sum, unit, False, F32, False)
        elif stage == "T":
            if c in SHARED:
                far_half[c] = merge(share[c], across[c])
            group = [(chunk, far_half[c])]
            oth_sum = matmul2(group, oth_sum, other, True, BF16 if c == last else F32, True)
            if c == last:
                back = lax.ppermute(oth_sum, "mode", KSWAP)
            own_sum = matmul2(group, own_sum, unit, False, F32, True)
        elif step == "G0":
            near = [(1, 0), (0, 3), (0, 1)]
            *vals, pick = gate([unit[u] for u in near], (1, 2))
            for u, v in zip(near, vals):
                unit[u] = v
                other[u] = lax.ppermute(v, "mode", KSWAP)
            unit[1, 3] = lax.ppermute(unit[1, 0], "cfg", cfg_perm(0, 1))
            unit[1, 1] = lax.ppermute(unit[1, 0], "cfg", cfg_perm(0, -1))
            unit[0, 2] = lax.ppermute(pick, ("cfg", "mode"), ONWARD)
        elif step == "G1":
            near = [(1, 3), (1, 1)]
            *vals, pick = gate([unit[u] for u in near], (0, 1))
            for u, v in zip(near, vals):
                unit[u] = v
                other[u] = lax.ppermute(v, "mode", KSWAP)
            unit[1, 2] = lax.ppermute(pick, ("cfg", "mode"), ONWARD)
        elif step == "G3":
            (f_far,) = gate([f_far])
        elif step == "G2":
            near = [(0, 2), (1, 2)]
            for u, v in zip(near, gate([unit[u] for u in near])):
                unit[u] = v
                other[u] = lax.ppermute(v, "mode", KSWAP)

    factor = weight[:, None] * (1.0 / math.sqrt(coords.shape[1] * lax.axis_size("cfg")))

    def finish(ins, outs, _):
        own, got = ins[1][...] * ins[0][...], wide(ins[2][...]) * ins[0][...]
        for c in range(2):

            @pl.when(place()[2] == c)
            def _():
                outs[0][:, :rows] = (own, got)[c]
                outs[0][:, rows:] = (got, own)[c]

    cut = FINISH if rows % (8 * FINISH) == 0 else 1
    shape = jax.ShapeDtypeStruct((rows, 2 * rows), F32)
    out = pl.pallas_call(
        lambda *refs: finish(refs[:3], refs[3:], ()),
        out_shape=shape,
        grid=(cut,),
        in_specs=[pl.BlockSpec((rows // cut, w), lambda t: (t, 0)) for w in (1, rows, rows)],
        out_specs=pl.BlockSpec((rows // cut, 2 * rows), lambda t: (t, 0)),
        compiler_params=pltpu.CompilerParams(vmem_limit_bytes=16 * 1024 * 1024),
        name="finish",
    )(factor, own_sum, back)
    return out.T


def solution(mesh):
    placed = (P("mode", "cfg"), P("mode"), P("mode"), P("mode", None), P("mode", "cfg"))
    return jax.shard_map(
        on_device, mesh=mesh, in_specs=placed, out_specs=P("cfg", "mode"), check_vma=False
    )
```

```python
import math

import jax
import jax.numpy as jnp
from jax import lax
from jax.experimental import pallas as pl
from jax.experimental.pallas import tpu as pltpu
from jax.sharding import PartitionSpec as P

F32 = jnp.float32
BF16 = jnp.bfloat16
X, Z = 4, 4
Q = 128
CHUNKS = (((0, 0), (0, 3), (0, 1), (1, 0)), ((1, 3), (1, 1)), ((0, 2), (1, 2)))
SHARED = (0,)
FINISH = 3
STEPS = (
    "G0", "G3", "M0", "G1", "M1", "S0", "G2", "Y0", "M2",
    "S1", "Y1", "S2", "R0", "R1", "F0", "Y2", "R2", "W0",
    "F1", "F2", "N2", "T1", "T0", "T2",
)


def mode_perm(fn):
    out = []
    for j in range(16):
        yl, x, k = j // 8, (j // 2) % 4, j % 2
        a, b, c = fn(yl, x, k)
        out.append((j, (a * 4 + b) * 2 + c))
    return out


FIRST = mode_perm(lambda yl, x, k: (yl, x ^ (3 if k else 1), k))
SECOND = mode_perm(lambda yl, x, k: (yl, x ^ (1 if k else 3), k))
YSWAP = mode_perm(lambda yl, x, k: (1 - yl, x, k))
KSWAP = mode_perm(lambda yl, x, k: (yl, x, 1 - k))


def all_perm(fn):
    out = []
    for d in range(128):
        src = (d // 64, (d // 16) % 4, (d // 8) % 2, (d // 2) % 4, d % 2)
        a, b, c, e, k = fn(*src)
        out.append((d, (((a * 4 + b) * 2 + c) * 4 + e) * 2 + k))
    return out


def cfg_perm(dy, dz):
    return [(c, (c // 4 ^ dy) * 4 + (c % 4 + dz) % 4) for c in range(8)]


ONWARD = all_perm(lambda yh, z, yl, x, k: (yh, (z + (3 if k else 1)) % 4, yl, x, k))
FORCES = all_perm(lambda yh, z, yl, x, k: (yl, x, yh, (x + z) % 4, k))

VM = pl.BlockSpec(memory_space=pltpu.VMEM)
SM = pl.BlockSpec(memory_space=pltpu.SMEM)
ANY = pl.BlockSpec(memory_space=pl.ANY)
HBM = pl.BlockSpec(memory_space=pltpu.HBM)
TOKEN = jax.ShapeDtypeStruct((8, 128), F32)


class Chain:
    def __init__(self):
        self.token = None
        self.step = ""

    def __call__(self, name, body, outs, args, specs, out_specs=None, aliases=None, scratch=(), mib=4):
        given = self.token is not None
        n_in, n_out = len(args), len(outs)

        def kernel(*refs):
            ins = refs[:n_in]
            rest = refs[n_in + int(given) :]
            rest[n_out][...] = jnp.zeros((8, 128), F32)
            body(ins, rest[:n_out], rest[n_out + 1 :])

        res = pl.pallas_call(
            kernel,
            out_shape=list(outs) + [TOKEN],
            in_specs=list(specs) + ([ANY] if given else []),
            out_specs=(list(out_specs) if out_specs else [VM] * n_out) + [VM],
            input_output_aliases=aliases or {},
            scratch_shapes=list(scratch),
            compiler_params=pltpu.CompilerParams(vmem_limit_bytes=mib * 1024 * 1024),
            cost_estimate=pl.CostEstimate(flops=1000, bytes_accessed=1000, transcendentals=0),
            name=self.step + name,
        )(*args, *([self.token] if given else []))
        self.token = res[-1]
        return res[:-1]


def like(v):
    return jax.ShapeDtypeStruct(v.shape, v.dtype)


def wide(v):
    return v.astype(F32)


def reorder(v):
    return jnp.concatenate([v[:, :Q], v[:, 2 * Q : 3 * Q], v[:, Q : 2 * Q], v[:, 3 * Q :]], axis=1)


def on_device(coords, curvature, weight, polar, forces):
    rows = coords.shape[0]
    run = Chain()

    def place():
        i, j = lax.axis_index("cfg"), lax.axis_index("mode")
        return i, j // 2, j % 2

    def pieces():
        _, chip, k = place()
        x = chip % X
        return x, x ^ (3 - 2 * k), x ^ (1 + 2 * k), x ^ 2

    def columns(piece):
        return pl.ds(pl.multiple_of(piece * Q, Q), Q)

    def arrange(v):
        def body(ins, outs, _):
            for s, p in enumerate(pieces()):
                outs[0][:, s * Q : (s + 1) * Q] = ins[0][:, columns(p)]

        return run("arrange", body, [like(v)], [v], [VM])[0]

    unit, other = {}, {}
    f_far = lax.ppermute(forces, ("cfg", "mode"), FORCES)
    unit[0, 0] = arrange(coords)
    other[0, 0] = lax.ppermute(unit[0, 0], "mode", KSWAP)
    unit[0, 3] = lax.ppermute(unit[0, 0], "cfg", cfg_perm(0, 1))
    unit[0, 1] = lax.ppermute(unit[0, 0], "cfg", cfg_perm(0, -1))
    unit[1, 0] = lax.ppermute(unit[0, 0], "cfg", cfg_perm(1, 0))

    window = 6 * 128

    def slice_polar(ins, outs, scratch):
        scale, source = ins
        i, _, k = place()
        wide_t, narrow, sems = scratch
        moves = []
        begins = [(2 * i + 1 - k) * rows, (2 * i + k) * rows]
        for h in range(2):
            begin = pl.multiple_of(begins[h] // 128 * 128, 128)
            moves.append(pltpu.make_async_copy(source.at[:, pl.ds(begin, window)], narrow.at[h], sems.at[h]))
            moves[-1].start()
        for h in range(2):
            moves[h].wait()
            wide_t[...] = wide(narrow[h]).T * scale[...][None, :]
            skip = pl.multiple_of(begins[h] % 128, 8)
            outs[h][...] = wide_t[pl.ds(skip, rows), :].astype(BF16)

    half = jax.ShapeDtypeStruct((rows, rows), BF16)
    px, po = run(
        "polar",
        slice_polar,
        [half, half],
        [curvature, polar],
        [VM, HBM],
        scratch=[
            pltpu.VMEM((window, rows), F32),
            pltpu.VMEM((2, rows, window), BF16),
            pltpu.SemaphoreType.DMA((2,)),
        ],
        mib=52,
    )
    px = lax.ppermute(px, "mode", KSWAP)

    def matmul1(chunk, f, early):
        n = len(chunk)
        shapes = [jax.ShapeDtypeStruct((rows, w * n * Q), BF16) for w in (1, 1, 2)]

        def body(ins, outs, _):
            a, b, fr = ins[:3]
            keep, s2, s1 = outs
            i, chip, _ = place()
            for u, (dy, dz) in enumerate(chunk):
                yh, z, yl, x = i // Z ^ dy, i % Z, chip // X, chip % X
                here = (i == chip) if early else (yh == yl) & ((2 * z + dz) % Z == x)
                flag = jnp.where(here, 1.0, 0.0)
                h = jnp.dot(a[...], ins[3 + 2 * u][...], preferred_element_type=F32)
                h += jnp.dot(b[...], reorder(ins[4 + 2 * u][...]), preferred_element_type=F32)
                part = [
                    (h[:, s * Q : (s + 1) * Q] + wide(fr[:, columns(p)]) * flag).astype(BF16)
                    for s, p in enumerate(pieces())
                ]
                lo, hi = slice(u * Q, (u + 1) * Q), slice((n + u) * Q, (n + u + 1) * Q)
                keep[:, lo] = part[0]
                s2[:, lo] = part[1]
                s1[:, lo] = part[2]
                s1[:, hi] = part[3]

        args = [po, px, f] + [v for u in chunk for v in (unit[u], other[u])]
        return run("product1", body, shapes, args, [VM] * len(args), mib=6 + 3 * n)

    def add(products, which, far, more=()):
        args = [v for p in products for v in (p[which], p[3])] + list(more)
        sizes = [p[which].shape[1] for p in products]

        def body(ins, outs, _):
            at = 0
            for q, w in enumerate(sizes):
                got = ins[2 * q + 1]
                total = wide(ins[2 * q][...]) + wide(got[:, w:] if far else got[:, :w])
                for r in ins[2 * len(sizes) :]:
                    total += wide(r[:, at : at + w])
                outs[0][:, at : at + w] = total.astype(BF16)
                at += w

        return run("add", body, [jax.ShapeDtypeStruct((rows, sum(sizes)), BF16)], args, [VM] * len(args), mib=6)[0]

    def add2(a, b):
        def body(ins, outs, _):
            outs[0][...] = (wide(ins[0][...]) + wide(ins[1][...])).astype(BF16)

        return run("add", body, [like(a)], [a, b], [VM] * 2)[0]

    def gate(args, pick=None):
        outs = [like(v) for v in args]
        scratch = []
        if pick:
            outs.append(like(args[pick[0]]))
            scratch = [pltpu.SemaphoreType.DMA]

        def body(ins, outs, sem):
            if pick:
                for c in range(2):

                    @pl.when(place()[2] == c)
                    def _():
                        move = pltpu.make_async_copy(ins[pick[c]], outs[-1], sem[0])
                        move.start()
                        move.wait()

        aliases = {a: a for a in range(len(args))}
        return run("gate", body, outs, list(args), [ANY] * len(args), [ANY] * len(outs), aliases, scratch)

    def join(a, b):
        w = a.shape[1]

        def body(ins, outs, _):
            outs[0][:, :w] = ins[0][...]
            outs[0][:, w:] = ins[1][...]

        return run("join", body, [jax.ShapeDtypeStruct((rows, 2 * w), BF16)], [a, b], [VM] * 2)[0]

    def is_low():
        return place()[1] // X == 0

    def join_and_pick(a, b):
        w = a.shape[1]

        def body(ins, outs, _):
            outs[0][:, :w] = ins[0][...]
            outs[0][:, w:] = ins[1][...]
            for side in range(2):

                @pl.when(is_low() == (side == 0))
                def _():
                    outs[1][...] = ins[side][...]

        shapes = [jax.ShapeDtypeStruct((rows, 2 * w), BF16), like(a)]
        return run("join", body, shapes, [a, b], [VM] * 2, mib=6)

    def merge(mine, across):
        w = mine.shape[1]

        def body(ins, outs, _):
            for side in range(2):

                @pl.when(is_low() == (side == 0))
                def _():
                    outs[0][:, :w] = ins[side][...]
                    outs[0][:, w:] = ins[1 - side][...]

        return run("merge", body, [jax.ShapeDtypeStruct((rows, 2 * w), BF16)], [mine, across], [VM] * 2, mib=6)[0]

    def matmul2(groups, acc, names, swap, dtype, far):
        begins = acc is None
        args = [] if begins else [acc]
        for chunk, r in groups:
            args += [r] + [names[u] for u in chunk]
        places = [(0, 2, 1, 3)[s] if swap else s for s in ((2, 3) if far else (0, 1))]

        def body(ins, outs, _):
            ins = list(ins)
            total = None if begins else ins.pop(0)[...]
            for chunk, _ in groups:
                n, r, ins = len(chunk), ins[0], ins[1:]
                for u in range(n):
                    ru = jnp.concatenate([r[:, (h * n + u) * Q : (h * n + u + 1) * Q] for h in range(2)], axis=1)
                    cu = jnp.concatenate([ins[u][:, p * Q : (p + 1) * Q] for p in places], axis=1)
                    t = lax.dot_general(cu, ru, (((1,), (1,)), ((), ())), preferred_element_type=F32)
                    total = t if total is None else total + t
                ins = ins[n:]
            outs[0][...] = total.astype(dtype)

        shape = jax.ShapeDtypeStruct((rows, rows), dtype)
        return run("product2", body, [shape], args, [VM] * len(args), mib=6 + 2 * sum(len(g[0]) for g in groups))[0]

    last = len(CHUNKS) - 1
    products = [[] for _ in CHUNKS]
    got2, part3, got3, r0, r1, near_half, far_half = ({} for _ in range(7))
    share, across = {}, {}
    own_sum = oth_sum = back = None
    begun = 0
    for step in STEPS:
        run.step = step.lower() + "_"
        stage, c = step[0], int(step[1])
        chunk = CHUNKS[c] if stage != "G" else ()
        if stage in "AM":
            early = stage == "A"
            part = chunk[:1] if early else chunk[len(products[c]) :]
            got = matmul1(part, forces if early else f_far, early)
            products[c].append((*got, lax.ppermute(got[2], "mode", FIRST)))
        elif stage == "S":
            v = add(products[c], 1, True)
            got2[c] = lax.ppermute(v, "mode", SECOND)
        elif stage == "Y":
            part3[c] = add(products[c], 0, False, [got2[c]])
            got3[c] = lax.ppermute(part3[c], "mode", YSWAP)
        elif stage == "R":
            r0[c] = add2(part3[c], got3[c])
            r1[c] = lax.ppermute(r0[c], "mode", SECOND)
        elif stage == "F":
            if c in SHARED:
                near_half[c], chosen = join_and_pick(r0[c], r1[c])
                share[c] = lax.ppermute(chosen, "mode", FIRST)
            else:
                near_half[c] = join(r0[c], r1[c])
                far_half[c] = lax.ppermute(near_half[c], "mode", FIRST)
        elif stage == "W":
            (share[c],) = gate([share[c]])
            across[c] = lax.ppermute(share[c], "mode", YSWAP)
        elif stage == "N":
            group = [(CHUNKS[d], near_half[d]) for d in range(begun, c + 1)]
            begun = c + 1
            oth_sum = matmul2(group, oth_sum, other, True, F32, False)
            own_sum = matmul2(group, own_sum, unit, False, F32, False)
        elif stage == "T":
            if c in SHARED:
                far_half[c] = merge(share[c], across[c])
            group = [(chunk, far_half[c])]
            oth_sum = matmul2(group, oth_sum, other, True, BF16 if c == last else F32, True)
            if c == last:
                back = lax.ppermute(oth_sum, "mode", KSWAP)
            own_sum = matmul2(group, own_sum, unit, False, F32, True)
        elif step == "G0":
            near = [(1, 0), (0, 3), (0, 1)]
            *vals, pick = gate([unit[u] for u in near], (1, 2))
            for u, v in zip(near, vals):
                unit[u] = v
                other[u] = lax.ppermute(v, "mode", KSWAP)
            unit[1, 3] = lax.ppermute(unit[1, 0], "cfg", cfg_perm(0, 1))
            unit[1, 1] = lax.ppermute(unit[1, 0], "cfg", cfg_perm(0, -1))
            unit[0, 2] = lax.ppermute(pick, ("cfg", "mode"), ONWARD)
        elif step == "G1":
            near = [(1, 3), (1, 1)]
            *vals, pick = gate([unit[u] for u in near], (0, 1))
            for u, v in zip(near, vals):
                unit[u] = v
                other[u] = lax.ppermute(v, "mode", KSWAP)
            unit[1, 2] = lax.ppermute(pick, ("cfg", "mode"), ONWARD)
        elif step == "G3":
            (f_far,) = gate([f_far])
        elif step == "G2":
            near = [(0, 2), (1, 2)]
            for u, v in zip(near, gate([unit[u] for u in near])):
                unit[u] = v
                other[u] = lax.ppermute(v, "mode", KSWAP)

    factor = weight[:, None] * (1.0 / math.sqrt(coords.shape[1] * lax.axis_size("cfg")))

    def finish(ins, outs, _):
        own, got = ins[1][...] * ins[0][...], wide(ins[2][...]) * ins[0][...]
        for c in range(2):

            @pl.when(place()[2] == c)
            def _():
                outs[0][:, :rows] = (own, got)[c]
                outs[0][:, rows:] = (got, own)[c]

    cut = FINISH if rows % (8 * FINISH) == 0 else 1
    shape = jax.ShapeDtypeStruct((rows, 2 * rows), F32)
    out = pl.pallas_call(
        lambda *refs: finish(refs[:3], refs[3:], ()),
        out_shape=shape,
        grid=(cut,),
        in_specs=[pl.BlockSpec((rows // cut, w), lambda t: (t, 0)) for w in (1, rows, rows)],
        out_specs=pl.BlockSpec((rows // cut, 2 * rows), lambda t: (t, 0)),
        compiler_params=pltpu.CompilerParams(vmem_limit_bytes=16 * 1024 * 1024),
        name="finish",
    )(factor, own_sum, back)
    return out.T


def solution(mesh):
    placed = (P("mode", "cfg"), P("mode"), P("mode"), P("mode", None), P("mode", "cfg"))
    return jax.shard_map(
        on_device, mesh=mesh, in_specs=placed, out_specs=P("cfg", "mode"), check_vma=False
    )
```

```python
import math

import jax
import jax.numpy as jnp
from jax import lax
from jax.experimental import pallas as pl
from jax.experimental.pallas import tpu as pltpu
from jax.sharding import PartitionSpec as P

F32 = jnp.float32
BF16 = jnp.bfloat16
X, Z = 4, 4
Q = 128
CHUNKS = (((0, 0), (0, 3), (0, 1), (1, 0)), ((1, 3), (1, 1)), ((0, 2), (1, 2)))
SHARED = (0,)
FINISH = 3
STEPS = (
    "G0", "G3", "M0", "G1", "M1", "S0", "G2", "Y0", "M2",
    "S1", "Y1", "S2", "R0", "R1", "F0", "Y2", "W0", "R2",
    "F1", "F2", "N2", "T1", "T0", "T2",
)


def mode_perm(fn):
    out = []
    for j in range(16):
        yl, x, k = j // 8, (j // 2) % 4, j % 2
        a, b, c = fn(yl, x, k)
        out.append((j, (a * 4 + b) * 2 + c))
    return out


FIRST = mode_perm(lambda yl, x, k: (yl, x ^ (3 if k else 1), k))
SECOND = mode_perm(lambda yl, x, k: (yl, x ^ (1 if k else 3), k))
YSWAP = mode_perm(lambda yl, x, k: (1 - yl, x, k))
KSWAP = mode_perm(lambda yl, x, k: (yl, x, 1 - k))


def all_perm(fn):
    out = []
    for d in range(128):
        src = (d // 64, (d // 16) % 4, (d // 8) % 2, (d // 2) % 4, d % 2)
        a, b, c, e, k = fn(*src)
        out.append((d, (((a * 4 + b) * 2 + c) * 4 + e) * 2 + k))
    return out


def cfg_perm(dy, dz):
    return [(c, (c // 4 ^ dy) * 4 + (c % 4 + dz) % 4) for c in range(8)]


ONWARD = all_perm(lambda yh, z, yl, x, k: (yh, (z + (3 if k else 1)) % 4, yl, x, k))
FORCES = all_perm(lambda yh, z, yl, x, k: (yl, x, yh, (x + z) % 4, k))

VM = pl.BlockSpec(memory_space=pltpu.VMEM)
SM = pl.BlockSpec(memory_space=pltpu.SMEM)
ANY = pl.BlockSpec(memory_space=pl.ANY)
HBM = pl.BlockSpec(memory_space=pltpu.HBM)
TOKEN = jax.ShapeDtypeStruct((8, 128), F32)


class Chain:
    def __init__(self):
        self.token = None
        self.step = ""

    def __call__(self, name, body, outs, args, specs, out_specs=None, aliases=None, scratch=(), mib=4):
        given = self.token is not None
        n_in, n_out = len(args), len(outs)

        def kernel(*refs):
            ins = refs[:n_in]
            rest = refs[n_in + int(given) :]
            rest[n_out][...] = jnp.zeros((8, 128), F32)
            body(ins, rest[:n_out], rest[n_out + 1 :])

        res = pl.pallas_call(
            kernel,
            out_shape=list(outs) + [TOKEN],
            in_specs=list(specs) + ([ANY] if given else []),
            out_specs=(list(out_specs) if out_specs else [VM] * n_out) + [VM],
            input_output_aliases=aliases or {},
            scratch_shapes=list(scratch),
            compiler_params=pltpu.CompilerParams(vmem_limit_bytes=mib * 1024 * 1024),
            cost_estimate=pl.CostEstimate(flops=1000, bytes_accessed=1000, transcendentals=0),
            name=self.step + name,
        )(*args, *([self.token] if given else []))
        self.token = res[-1]
        return res[:-1]


def like(v):
    return jax.ShapeDtypeStruct(v.shape, v.dtype)


def wide(v):
    return v.astype(F32)


def reorder(v):
    return jnp.concatenate([v[:, :Q], v[:, 2 * Q : 3 * Q], v[:, Q : 2 * Q], v[:, 3 * Q :]], axis=1)


def on_device(coords, curvature, weight, polar, forces):
    rows = coords.shape[0]
    run = Chain()

    def place():
        i, j = lax.axis_index("cfg"), lax.axis_index("mode")
        return i, j // 2, j % 2

    def pieces():
        _, chip, k = place()
        x = chip % X
        return x, x ^ (3 - 2 * k), x ^ (1 + 2 * k), x ^ 2

    def columns(piece):
        return pl.ds(pl.multiple_of(piece * Q, Q), Q)

    def arrange(v):
        def body(ins, outs, _):
            for s, p in enumerate(pieces()):
                outs[0][:, s * Q : (s + 1) * Q] = ins[0][:, columns(p)]

        return run("arrange", body, [like(v)], [v], [VM])[0]

    unit, other = {}, {}
    f_far = lax.ppermute(forces, ("cfg", "mode"), FORCES)
    unit[0, 0] = arrange(coords)
    other[0, 0] = lax.ppermute(unit[0, 0], "mode", KSWAP)
    unit[0, 3] = lax.ppermute(unit[0, 0], "cfg", cfg_perm(0, 1))
    unit[0, 1] = lax.ppermute(unit[0, 0], "cfg", cfg_perm(0, -1))
    unit[1, 0] = lax.ppermute(unit[0, 0], "cfg", cfg_perm(1, 0))

    window = 6 * 128

    def slice_polar(ins, outs, scratch):
        scale, source = ins
        i, _, k = place()
        wide_t, narrow, sems = scratch
        moves = []
        begins = [(2 * i + 1 - k) * rows, (2 * i + k) * rows]
        for h in range(2):
            begin = pl.multiple_of(begins[h] // 128 * 128, 128)
            moves.append(pltpu.make_async_copy(source.at[:, pl.ds(begin, window)], narrow.at[h], sems.at[h]))
            moves[-1].start()
        for h in range(2):
            moves[h].wait()
            wide_t[...] = wide(narrow[h]).T * scale[...][None, :]
            skip = pl.multiple_of(begins[h] % 128, 8)
            outs[h][...] = wide_t[pl.ds(skip, rows), :].astype(BF16)

    half = jax.ShapeDtypeStruct((rows, rows), BF16)
    px, po = run(
        "polar",
        slice_polar,
        [half, half],
        [curvature, polar],
        [VM, HBM],
        scratch=[
            pltpu.VMEM((window, rows), F32),
            pltpu.VMEM((2, rows, window), BF16),
            pltpu.SemaphoreType.DMA((2,)),
        ],
        mib=52,
    )
    px = lax.ppermute(px, "mode", KSWAP)

    def matmul1(chunk, f, early):
        n = len(chunk)
        shapes = [jax.ShapeDtypeStruct((rows, w * n * Q), BF16) for w in (1, 1, 2)]

        def body(ins, outs, _):
            a, b, fr = ins[:3]
            keep, s2, s1 = outs
            i, chip, _ = place()
            for u, (dy, dz) in enumerate(chunk):
                yh, z, yl, x = i // Z ^ dy, i % Z, chip // X, chip % X
                here = (i == chip) if early else (yh == yl) & ((2 * z + dz) % Z == x)
                flag = jnp.where(here, 1.0, 0.0)
                h = jnp.dot(a[...], ins[3 + 2 * u][...], preferred_element_type=F32)
                h += jnp.dot(b[...], reorder(ins[4 + 2 * u][...]), preferred_element_type=F32)
                part = [
                    (h[:, s * Q : (s + 1) * Q] + wide(fr[:, columns(p)]) * flag).astype(BF16)
                    for s, p in enumerate(pieces())
                ]
                lo, hi = slice(u * Q, (u + 1) * Q), slice((n + u) * Q, (n + u + 1) * Q)
                keep[:, lo] = part[0]
                s2[:, lo] = part[1]
                s1[:, lo] = part[2]
                s1[:, hi] = part[3]

        args = [po, px, f] + [v for u in chunk for v in (unit[u], other[u])]
        return run("product1", body, shapes, args, [VM] * len(args), mib=6 + 3 * n)

    def add(products, which, far, more=()):
        args = [v for p in products for v in (p[which], p[3])] + list(more)
        sizes = [p[which].shape[1] for p in products]

        def body(ins, outs, _):
            at = 0
            for q, w in enumerate(sizes):
                got = ins[2 * q + 1]
                total = wide(ins[2 * q][...]) + wide(got[:, w:] if far else got[:, :w])
                for r in ins[2 * len(sizes) :]:
                    total += wide(r[:, at : at + w])
                outs[0][:, at : at + w] = total.astype(BF16)
                at += w

        return run("add", body, [jax.ShapeDtypeStruct((rows, sum(sizes)), BF16)], args, [VM] * len(args), mib=6)[0]

    def add2(a, b):
        def body(ins, outs, _):
            outs[0][...] = (wide(ins[0][...]) + wide(ins[1][...])).astype(BF16)

        return run("add", body, [like(a)], [a, b], [VM] * 2)[0]

    def gate(args, pick=None):
        outs = [like(v) for v in args]
        scratch = []
        if pick:
            outs.append(like(args[pick[0]]))
            scratch = [pltpu.SemaphoreType.DMA]

        def body(ins, outs, sem):
            if pick:
                for c in range(2):

                    @pl.when(place()[2] == c)
                    def _():
                        move = pltpu.make_async_copy(ins[pick[c]], outs[-1], sem[0])
                        move.start()
                        move.wait()

        aliases = {a: a for a in range(len(args))}
        return run("gate", body, outs, list(args), [ANY] * len(args), [ANY] * len(outs), aliases, scratch)

    def join(a, b):
        w = a.shape[1]

        def body(ins, outs, _):
            outs[0][:, :w] = ins[0][...]
            outs[0][:, w:] = ins[1][...]

        return run("join", body, [jax.ShapeDtypeStruct((rows, 2 * w), BF16)], [a, b], [VM] * 2)[0]

    def is_low():
        return place()[1] // X == 0

    def join_and_pick(a, b):
        w = a.shape[1]

        def body(ins, outs, _):
            outs[0][:, :w] = ins[0][...]
            outs[0][:, w:] = ins[1][...]
            for side in range(2):

                @pl.when(is_low() == (side == 0))
                def _():
                    outs[1][...] = ins[side][...]

        shapes = [jax.ShapeDtypeStruct((rows, 2 * w), BF16), like(a)]
        return run("join", body, shapes, [a, b], [VM] * 2, mib=6)

    def merge(mine, across):
        w = mine.shape[1]

        def body(ins, outs, _):
            for side in range(2):

                @pl.when(is_low() == (side == 0))
                def _():
                    outs[0][:, :w] = ins[side][...]
                    outs[0][:, w:] = ins[1 - side][...]

        return run("merge", body, [jax.ShapeDtypeStruct((rows, 2 * w), BF16)], [mine, across], [VM] * 2, mib=6)[0]

    def matmul2(groups, acc, names, swap, dtype, far):
        begins = acc is None
        args = [] if begins else [acc]
        for chunk, r in groups:
            args += [r] + [names[u] for u in chunk]
        places = [(0, 2, 1, 3)[s] if swap else s for s in ((2, 3) if far else (0, 1))]

        def body(ins, outs, _):
            ins = list(ins)
            total = None if begins else ins.pop(0)[...]
            for chunk, _ in groups:
                n, r, ins = len(chunk), ins[0], ins[1:]
                for u in range(n):
                    ru = jnp.concatenate([r[:, (h * n + u) * Q : (h * n + u + 1) * Q] for h in range(2)], axis=1)
                    cu = jnp.concatenate([ins[u][:, p * Q : (p + 1) * Q] for p in places], axis=1)
                    t = lax.dot_general(cu, ru, (((1,), (1,)), ((), ())), preferred_element_type=F32)
                    total = t if total is None else total + t
                ins = ins[n:]
            outs[0][...] = total.astype(dtype)

        shape = jax.ShapeDtypeStruct((rows, rows), dtype)
        return run("product2", body, [shape], args, [VM] * len(args), mib=6 + 2 * sum(len(g[0]) for g in groups))[0]

    last = len(CHUNKS) - 1
    products = [[] for _ in CHUNKS]
    got2, part3, got3, r0, r1, near_half, far_half = ({} for _ in range(7))
    share, across = {}, {}
    own_sum = oth_sum = back = None
    begun = 0
    for step in STEPS:
        run.step = step.lower() + "_"
        stage, c = step[0], int(step[1])
        chunk = CHUNKS[c] if stage != "G" else ()
        if stage in "AM":
            early = stage == "A"
            part = chunk[:1] if early else chunk[len(products[c]) :]
            got = matmul1(part, forces if early else f_far, early)
            products[c].append((*got, lax.ppermute(got[2], "mode", FIRST)))
        elif stage == "S":
            v = add(products[c], 1, True)
            got2[c] = lax.ppermute(v, "mode", SECOND)
        elif stage == "Y":
            part3[c] = add(products[c], 0, False, [got2[c]])
            got3[c] = lax.ppermute(part3[c], "mode", YSWAP)
        elif stage == "R":
            r0[c] = add2(part3[c], got3[c])
            r1[c] = lax.ppermute(r0[c], "mode", SECOND)
        elif stage == "F":
            if c in SHARED:
                near_half[c], chosen = join_and_pick(r0[c], r1[c])
                share[c] = lax.ppermute(chosen, "mode", FIRST)
            else:
                near_half[c] = join(r0[c], r1[c])
                far_half[c] = lax.ppermute(near_half[c], "mode", FIRST)
        elif stage == "W":
            (share[c],) = gate([share[c]])
            across[c] = lax.ppermute(share[c], "mode", YSWAP)
        elif stage == "N":
            group = [(CHUNKS[d], near_half[d]) for d in range(begun, c + 1)]
            begun = c + 1
            oth_sum = matmul2(group, oth_sum, other, True, F32, False)
            own_sum = matmul2(group, own_sum, unit, False, F32, False)
        elif stage == "T":
            if c in SHARED:
                far_half[c] = merge(share[c], across[c])
            group = [(chunk, far_half[c])]
            oth_sum = matmul2(group, oth_sum, other, True, BF16 if c == last else F32, True)
            if c == last:
                back = lax.ppermute(oth_sum, "mode", KSWAP)
            own_sum = matmul2(group, own_sum, unit, False, F32, True)
        elif step == "G0":
            near = [(1, 0), (0, 3), (0, 1)]
            *vals, pick = gate([unit[u] for u in near], (1, 2))
            for u, v in zip(near, vals):
                unit[u] = v
                other[u] = lax.ppermute(v, "mode", KSWAP)
            unit[1, 3] = lax.ppermute(unit[1, 0], "cfg", cfg_perm(0, 1))
            unit[1, 1] = lax.ppermute(unit[1, 0], "cfg", cfg_perm(0, -1))
            unit[0, 2] = lax.ppermute(pick, ("cfg", "mode"), ONWARD)
        elif step == "G1":
            near = [(1, 3), (1, 1)]
            *vals, pick = gate([unit[u] for u in near], (0, 1))
            for u, v in zip(near, vals):
                unit[u] = v
                other[u] = lax.ppermute(v, "mode", KSWAP)
            unit[1, 2] = lax.ppermute(pick, ("cfg", "mode"), ONWARD)
        elif step == "G3":
            (f_far,) = gate([f_far])
        elif step == "G2":
            near = [(0, 2), (1, 2)]
            for u, v in zip(near, gate([unit[u] for u in near])):
                unit[u] = v
                other[u] = lax.ppermute(v, "mode", KSWAP)

    factor = weight[:, None] * (1.0 / math.sqrt(coords.shape[1] * lax.axis_size("cfg")))

    def finish(ins, outs, _):
        own, got = ins[1][...] * ins[0][...], wide(ins[2][...]) * ins[0][...]
        for c in range(2):

            @pl.when(place()[2] == c)
            def _():
                outs[0][:, :rows] = (own, got)[c]
                outs[0][:, rows:] = (got, own)[c]

    cut = FINISH if rows % (8 * FINISH) == 0 else 1
    shape = jax.ShapeDtypeStruct((rows, 2 * rows), F32)
    out = pl.pallas_call(
        lambda *refs: finish(refs[:3], refs[3:], ()),
        out_shape=shape,
        grid=(cut,),
        in_specs=[pl.BlockSpec((rows // cut, w), lambda t: (t, 0)) for w in (1, rows, rows)],
        out_specs=pl.BlockSpec((rows // cut, 2 * rows), lambda t: (t, 0)),
        compiler_params=pltpu.CompilerParams(vmem_limit_bytes=16 * 1024 * 1024),
        name="finish",
    )(factor, own_sum, back)
    return out.T


def solution(mesh):
    placed = (P("mode", "cfg"), P("mode"), P("mode"), P("mode", None), P("mode", "cfg"))
    return jax.shard_map(
        on_device, mesh=mesh, in_specs=placed, out_specs=P("cfg", "mode"), check_vma=False
    )
```
